32 devices in a mesh: dp: 2 (over core), gx: 16 (over z, y, x).
Axes of the slice: x: 2, y: 2, z: 4, core: 2. Of those that a mesh axis runs over, the one named last changes fastest.
Arguments:
- features: bfloat16 [2, 16, 32, 8, 256], P('dp', None, 'gx'), may hold values from -6 to 6
- offsets: int32 [2, 3], P('dp'), may hold values from 0 to 255, as said below
- flip_bits: int32 [2, 3], P('dp'), may hold values from 0 to 1
- weight: bfloat16 [27, 16, 16], replicated, may hold values from -0.3125 to 0.3125
- conv_bias: float32 [16], replicated, may hold values from -3 to 3
- cotangent: bfloat16 [2, 16, 32, 8, 256], P('dp', None, 'gx'), may hold values from -6 to 6
Outputs:
- hidden: bfloat16 [2, 16, 32, 8, 256], P('dp', None, 'gx')
- grad_input: bfloat16 [2, 16, 32, 8, 256], P('dp', None, 'gx')
- grad_weight: float32 [27, 16, 16], replicated
- grad_bias: float32 [16], replicated
The draws below stay inside these ranges and needn't reach their ends.
Inputs may be any that keep to these rules, and one draw needn't show every extreme that they name: `offsets`: column 0 lies in 0 to 31, column 1 in 0 to 7, column 2 in 0 to 255.
All inputs are finite; a program needn't handle non-finite values.
Results may differ from the reference program's by a relative error of at most 0.0075.
Values may be sent and summed in bfloat16 or wider, within the bound.
A program may use at most 64 MiB of HBM per device.

```python
import math
import jax
import jax.numpy as jnp
from jax import lax

CH = 16
NY = 8
NZ = 256
NX = 32
FIELDS = 2


def draw_offsets(key, part):
    limits = jnp.array([NX, NY, NZ], dtype=jnp.int32)
    drawn = jax.random.randint(jax.random.fold_in(key, 1), (FIELDS, 3), 0, limits, dtype=jnp.int32)
    field_high = jax.random.randint(jax.random.fold_in(key, 2), (), 0, FIELDS, dtype=jnp.int32)
    field_low = jnp.mod(field_high + 1, FIELDS).astype(jnp.int32)
    rows = jnp.arange(FIELDS, dtype=jnp.int32)[:, None]
    columns = jnp.arange(3, dtype=jnp.int32)[None, :]
    drawn = jnp.where(rows == field_high, (limits - 1)[None, :], drawn)
    drawn = jnp.where((rows == field_low) & (columns == 2), jnp.zeros_like(drawn), drawn)
    return drawn.astype(jnp.int32)


def touch_ends(values, rng, smallest, high):
    place = [jax.random.randint(jax.random.fold_in(rng, axis), (), 0, length) for axis, length in enumerate(values.shape)]
    longest = values.shape.index(max(values.shape))
    next_to = place[:longest] + [(place[longest] + 1) % values.shape[longest]] + place[longest + 1:]
    return values.at[tuple(place)].set(smallest).at[tuple(next_to)].set(high)


def steps_of(own_key, extent, shards, least, largest):
    gain = 1.0
    for dim, blocks in shards:
        draws = jax.random.uniform(jax.random.fold_in(jax.random.fold_in(own_key, 6), dim), (blocks,), jnp.float32, least / len(shards), largest / len(shards))
        gain = gain * jnp.repeat(jnp.exp(draws), extent[dim] // blocks).reshape((-1,) + (1,) * (len(extent) - 1 - dim))
    return gain


def bell_draw(stream_key, dims, deviation, most, pieces=(), kind=jnp.bfloat16):
    result = jax.random.normal(stream_key, dims, jnp.float32) * deviation
    if len(pieces) > 0:
        result = steps_of(stream_key, dims, pieces, -0.22, 0.18) * result
    return jnp.clip(result, min=-most, max=most).astype(kind)


def setup_inputs(seed: int = 0) -> dict:
    key_list = jax.random.split(jax.random.key(seed), 7)
    return {
        "features": bell_draw(key_list[0], (FIELDS, CH, NX, NY, NZ), 1.0, 6.0, ((0, 2), (2, 16))),
        "offsets": draw_offsets(jax.random.fold_in(key_list[6], 71), 0),
        "flip_bits": touch_ends(jax.random.randint(key_list[2], (FIELDS, 3), 0, 2), jax.random.fold_in(key_list[2], 1), 0, 1).astype(jnp.int32),
        "weight": bell_draw(key_list[3], (27, CH, CH), (27 * CH) ** -0.5, 0.3125),
        "conv_bias": bell_draw(key_list[4], (CH,), 0.5, 3.0, (), jnp.float32),
        "cotangent": bell_draw(key_list[5], (FIELDS, CH, NX, NY, NZ), 1.0, 6.0, ((0, 2), (2, 16))),
    }


tap_offsets = [(shift_x, shift_y, shift_z) for shift_x in range(3) for shift_y in range(3) for shift_z in range(3)]

def permute_axis(volume, offset, mirror_bit, length, dim_index):
    position = jnp.arange(length, dtype=jnp.int32)
    source = jnp.where(mirror_bit == 1, length - 1 - position, position)
    source = jnp.mod(source - offset, length).astype(jnp.int32)
    return jnp.take(volume, source, axis=dim_index)

def gelu_parts(pre_act):
    normal_cdf = 0.5 * (1.0 + lax.erf(pre_act * 0.7071067811865476))
    density = jnp.exp(-0.5 * pre_act * pre_act) * 0.3989422804014327
    return (pre_act * normal_cdf, normal_cdf + pre_act * density)

def one_field(volume, offset, mirror_bits, cotangent, weight, conv_bias):
    augmented = permute_axis(volume, offset[0], mirror_bits[0], NX, 1)
    augmented = permute_axis(augmented, offset[1], mirror_bits[1], NY, 2)
    augmented = permute_axis(augmented, offset[2], mirror_bits[2], NZ, 3)
    augmented32 = augmented.astype(jnp.float32)
    weights32 = weight.astype(jnp.float32)
    total = jnp.zeros(augmented32.shape, jnp.float32) + conv_bias.astype(jnp.float32)[:, None, None, None]
    for tap_index, (shift_x, shift_y, shift_z) in enumerate(tap_offsets):
        window = jnp.roll(augmented32, (1 - shift_x, 1 - shift_y, 1 - shift_z), axis=(1, 2, 3))
        total = total + jnp.einsum('oi,ixyz->oxyz', weights32[tap_index], window)
    hidden, slope = gelu_parts(total)
    grad_pre = (cotangent.astype(jnp.float32) * slope).astype(jnp.bfloat16)
    grad32 = grad_pre.astype(jnp.float32)
    grad_in = jnp.zeros(augmented32.shape, jnp.float32)
    grad_list = []
    for tap_index, (shift_x, shift_y, shift_z) in enumerate(tap_offsets):
        window = jnp.roll(augmented32, (1 - shift_x, 1 - shift_y, 1 - shift_z), axis=(1, 2, 3))
        grad_list.append(jnp.einsum('oxyz,ixyz->oi', grad32, window))
        moved_grad = jnp.roll(grad32, (shift_x - 1, shift_y - 1, shift_z - 1), axis=(1, 2, 3))
        grad_in = grad_in + jnp.einsum('oi,oxyz->ixyz', weights32[tap_index], moved_grad)
    return (hidden.astype(jnp.bfloat16), grad_in.astype(jnp.bfloat16), jnp.stack(grad_list), lax.optimization_barrier(jnp.sum(grad32, axis=(1, 2, 3))))

def reference(features, offsets, flip_bits, weight, conv_bias, cotangent):

    def run_field(items):
        return one_field(items[0], items[1], items[2], items[3], weight, conv_bias)
    hidden, grad_input, grad_w, grad_b = lax.map(run_field, (features, offsets, flip_bits, cotangent))
    grad_scale = 1.0 / math.sqrt(FIELDS * NX * NY * NZ)
    return (hidden, grad_input, lax.optimization_barrier(jnp.sum(grad_w, axis=0)) * grad_scale, lax.optimization_barrier(jnp.sum(grad_b, axis=0)) * grad_scale)
```

```python
import functools
import math

import jax
import jax.numpy as jnp
from jax import lax
from jax.experimental import pallas as pl
from jax.experimental.pallas import tpu as pltpu
from jax.sharding import PartitionSpec as P

MESH = pl.DeviceIdType.MESH
bf16, f32 = jnp.bfloat16, jnp.float32


def iota(shape, dim):
    return lax.broadcasted_iota(jnp.int32, shape, dim)


def one_hot(mask):
    return jnp.where(mask, 1.0, 0.0).astype(bf16)


def mm(a, b):
    return jnp.dot(a, b, preferred_element_type=f32)


def mm_t(a, b):
    return lax.dot_general(a, b, (((1,), (1,)), ((), ())), preferred_element_type=f32)


def gelu_parts(pre_act):
    normal_cdf = 0.5 * (1.0 + lax.erf(pre_act * 0.7071067811865476))
    density = jnp.exp(-0.5 * pre_act * pre_act) * 0.3989422804014327
    return (pre_act * normal_cdf, normal_cdf + pre_act * density)


def wait_bytes(ref, sem):
    pltpu.make_async_copy(ref, ref, sem).wait()


def kernel(
    n, dps, planes, ch, ny, nz, scale,
    off_ref, flip_ref, feat_ref, weight_ref, bias_ref, cot_ref,
    hid_ref, gin_ref, gw_ref,
    send1, recv1, stag, recv2, cols, gcols, gext, rs, rsr, dpr, ag,
    send_sems, recv_sems,
):
    me, my_dp = lax.axis_index("gx"), lax.axis_index("dp")
    taps = 27
    rows = ch * planes * ny
    chunks = ny * nz // 128
    nx = n * planes
    per = rs.shape[1]

    barrier = pltpu.get_barrier_semaphore()

    def greet(k, _):
        pl.semaphore_signal(
            barrier, inc=1, device_id={"gx": lax.rem(me + k, n)}, device_id_type=MESH
        )
        return 0

    def greet_dp(k, _):
        pl.semaphore_signal(
            barrier, inc=1, device_id={"dp": lax.rem(my_dp + k, dps)}, device_id_type=MESH
        )
        return 0

    lax.fori_loop(1, n, greet, 0)
    lax.fori_loop(1, dps, greet_dp, 0)

    r_out = iota((rows, rows), 0)
    r_in = iota((rows, rows), 1)
    out_c, out_y, out_x = r_out % ch, (r_out // ch) % ny, r_out // (ch * ny)
    base = (out_c * planes + out_x) * ny
    src_y = jnp.where(flip_ref[0, 1] == 1, ny - 1 - out_y, out_y) - off_ref[0, 1]
    src_y = jnp.bitwise_and(src_y, ny - 1)
    order = one_hot(r_in == base + out_y)
    order_aug = one_hot(r_in == base + src_y)
    zi, zo = iota((nz, nz), 0), iota((nz, nz), 1)
    src_z = jnp.where(flip_ref[0, 2] == 1, nz - 1 - zo, zo) - off_ref[0, 2]
    perm_z = one_hot(zi == jnp.bitwise_and(src_z, nz - 1))
    local = mm(feat_ref[...], perm_z).astype(bf16)
    local = mm(order_aug, local).astype(bf16)
    for j in range(chunks):
        y, half = j // 2, j % 2
        for x in range(planes):
            r0 = (x * ny + y) * ch
            send1[j, x] = local[r0 : r0 + ch, half * 128 : half * 128 + 128]

    pl.semaphore_wait(barrier, n + dps - 2)

    def start1(k, _):
        peer = lax.rem(me + k, n)
        pltpu.make_async_remote_copy(
            src_ref=send1.at[lax.rem(peer, chunks)],
            dst_ref=recv1.at[pl.ds(me * planes, planes)],
            send_sem=send_sems.at[0],
            recv_sem=recv_sems.at[0],
            device_id={"gx": peer},
            device_id_type=MESH,
        ).start()
        return 0

    lax.fori_loop(1, n, start1, 0)
    my_chunk = lax.rem(me, chunks)
    group = me // chunks * chunks
    recv1[pl.ds(me * planes, planes)] = send1[my_chunk]

    width = taps * ch
    w2 = weight_ref[...]
    spread = mm(w2, one_hot(iota((ch, width), 0) == iota((ch, width), 1) % ch))
    same_tap = iota((width, width), 0) // ch == iota((width, width), 1) // ch
    spread = jnp.where(same_tap, spread, 0.0).astype(bf16)
    gather = one_hot(iota((ch, width), 0) == iota((ch, width), 1) % ch)
    w_fwd = mm(gather, spread).astype(bf16)
    eye = one_hot(iota((ch, ch), 0) == iota((ch, ch), 1))
    w_bwd = mm_t(eye, w2).astype(bf16)
    cot = mm(order, cot_ref[...])
    bias = bias_ref[...]
    z_less = one_hot(zi == jnp.bitwise_and(zo - 1, nz - 1))
    z_more = one_hot(zi == jnp.bitwise_and(zo + 1, nz - 1))
    cols[width : width + ch] = jnp.ones((ch, cols.shape[1]), bf16)

    wait_bytes(recv1.at[pl.ds(0, (n - 1) * planes)], recv_sems.at[0])

    for p in range(chunks * planes + 2):
        target = lax.rem(group * planes + (p - 1 + nx), nx)
        source = jnp.where(flip_ref[0, 0] == 1, nx - 1 - target, target) - off_ref[0, 0]
        stag[p] = recv1[lax.rem(source + nx, nx)]

    def start2(k, _):
        q = lax.rem(my_chunk + k, chunks)
        pltpu.make_async_remote_copy(
            src_ref=stag.at[pl.ds(q * planes, planes + 2)],
            dst_ref=recv2.at[my_chunk],
            send_sem=send_sems.at[1],
            recv_sem=recv_sems.at[1],
            device_id={"gx": group + q},
            device_id_type=MESH,
        ).start()
        return 0

    lax.fori_loop(1, chunks, start2, 0)
    recv2[my_chunk] = stag[pl.ds(my_chunk * planes, planes + 2)]
    wait_bytes(recv2.at[pl.ds(0, chunks - 1)], recv_sems.at[1])

    def lane(x, y):
        return (x * ny + y) * nz

    for p in range(planes + 2):
        mid = [
            jnp.concatenate([recv2[2 * y, p], recv2[2 * y + 1, p]], axis=1) for y in range(ny)
        ]
        stacked = jnp.concatenate(mid, axis=0)
        shifts = [mm(stacked, z_less).astype(bf16), stacked, mm(stacked, z_more).astype(bf16)]
        for a in range(3):
            x = p - a
            if not 0 <= x < planes:
                continue
            for e in range(3):
                for h in range(3):
                    t = 9 * a + 3 * e + h
                    for y in range(ny):
                        s = (y + e - 1) % ny
                        cols[t * ch : t * ch + ch, lane(x, y) : lane(x, y) + nz] = shifts[h][
                            s * ch : s * ch + ch
                        ]

    hidden = []
    for x in range(planes):
        for y in range(ny):
            r0 = (x * ny + y) * ch
            at = slice(lane(x, y), lane(x, y) + nz)
            pre = mm(w_fwd, cols[0:width, at]) + bias
            act, slope = gelu_parts(pre)
            hidden.append(act.astype(bf16))
            gext[x + 1, y] = (cot[r0 : r0 + ch] * slope).astype(bf16)

    right, left = lax.rem(me + 1, n), lax.rem(me + n - 1, n)
    halos = [
        pltpu.make_async_remote_copy(
            src_ref=gext.at[here],
            dst_ref=gext.at[there],
            send_sem=send_sems.at[2 + side],
            recv_sem=recv_sems.at[2 + side],
            device_id={"gx": peer},
            device_id_type=MESH,
        )
        for side, (here, there, peer) in enumerate(
            [(planes, 0, right), (1, planes + 1, left)]
        )
    ]
    for halo in halos:
        halo.start()

    gw = jnp.zeros((ch, width + ch), f32)
    for x in range(planes):
        for y in range(ny):
            gw = gw + mm_t(gext[x + 1, y], cols[:, lane(x, y) : lane(x, y) + nz])
    gw = jnp.concatenate([gw, jnp.zeros((ch, 512 - width - ch), f32)], axis=1)
    groups = ch // per
    for k in range(n):
        g, q = k % groups, k // groups
        rs[k] = gw[g * per : g * per + per, q * 128 : q * 128 + 128]

    def start_rs(k, _):
        peer = lax.rem(me + k, n)
        pltpu.make_async_remote_copy(
            src_ref=rs.at[peer],
            dst_ref=rsr.at[me],
            send_sem=send_sems.at[4],
            recv_sem=recv_sems.at[4],
            device_id={"gx": peer},
            device_id_type=MESH,
        ).start()
        return 0

    lax.fori_loop(1, n, start_rs, 0)
    rsr[me] = rs[me]

    hid_ref[...] = lax.dot_general(
        order, jnp.concatenate(hidden, axis=0), (((0,), (0,)), ((), ())),
        preferred_element_type=f32,
    ).astype(bf16)

    def grad_columns(p):
        stacked = jnp.concatenate([gext[p, y] for y in range(ny)], axis=0)
        shifts = [mm(stacked, z_more).astype(bf16), stacked, mm(stacked, z_less).astype(bf16)]
        for a in range(3):
            x = p + a - 2
            if not 0 <= x < planes:
                continue
            for e in range(3):
                for h in range(3):
                    t = 9 * a + 3 * e + h
                    for y in range(ny):
                        s = (y + 1 - e) % ny
                        gcols[t * ch : t * ch + ch, lane(x, y) : lane(x, y) + nz] = shifts[h][
                            s * ch : s * ch + ch
                        ]

    for p in range(1, planes + 1):
        grad_columns(p)

    wait_bytes(rsr.at[pl.ds(0, n - 1)], recv_sems.at[4])
    total = rsr[0]
    for k in range(1, n):
        total = total + rsr[k]
    dpr[my_dp] = total

    def start_dp(k, _):
        pltpu.make_async_remote_copy(
            src_ref=dpr.at[my_dp],
            dst_ref=dpr.at[my_dp],
            send_sem=send_sems.at[5],
            recv_sem=recv_sems.at[5],
            device_id={"dp": lax.rem(my_dp + k, dps)},
            device_id_type=MESH,
        ).start()
        return 0

    lax.fori_loop(1, dps, start_dp, 0)

    for halo in halos:
        halo.wait()
    grad_columns(0)
    grad_columns(planes + 1)

    wait_bytes(dpr.at[pl.ds(0, dps - 1)], recv_sems.at[5])
    total = dpr[0]
    for k in range(1, dps):
        total = total + dpr[k]
    ag[me] = total * scale

    def start_ag(k, _):
        pltpu.make_async_remote_copy(
            src_ref=ag.at[me],
            dst_ref=ag.at[me],
            send_sem=send_sems.at[6],
            recv_sem=recv_sems.at[6],
            device_id={"gx": lax.rem(me + k, n)},
            device_id_type=MESH,
        ).start()
        return 0

    lax.fori_loop(1, n, start_ag, 0)

    grad_in = [
        mm(w_bwd, gcols[:, lane(x, y) : lane(x, y) + nz]).astype(bf16)
        for x in range(planes)
        for y in range(ny)
    ]
    gin_ref[...] = lax.dot_general(
        order, jnp.concatenate(grad_in, axis=0), (((0,), (0,)), ((), ())),
        preferred_element_type=f32,
    ).astype(bf16)

    wait_bytes(ag.at[pl.ds(0, n - 1)], recv_sems.at[6])
    for k in range(n):
        g, q = k % groups, k // groups
        gw_ref[g * per : g * per + per, q * 128 : q * 128 + 128] = ag[k]

    wait_bytes(recv1.at[pl.ds(0, (n - 1) * planes)], send_sems.at[0])
    wait_bytes(recv2.at[pl.ds(0, chunks - 1)], send_sems.at[1])
    wait_bytes(rsr.at[pl.ds(0, n - 1)], send_sems.at[4])
    wait_bytes(dpr.at[pl.ds(0, dps - 1)], send_sems.at[5])
    wait_bytes(ag.at[pl.ds(0, n - 1)], send_sems.at[6])


def on_device(features, offsets, flip_bits, weight, conv_bias, cotangent):
    _, ch, planes, ny, nz = features.shape
    n, dps = lax.axis_size("gx"), lax.axis_size("dp")
    taps = weight.shape[0]
    rows, cells, chunks = ch * planes * ny, planes * ny * nz, ny * nz // 128
    width = taps * ch
    per = ch * 512 // (128 * n)
    scale = 1.0 / math.sqrt(dps * n * cells)
    vmem = pl.BlockSpec(memory_space=pltpu.VMEM)
    smem = pl.BlockSpec(memory_space=pltpu.SMEM)
    hidden, grad_in, grad_w = pl.pallas_call(
        functools.partial(kernel, n, dps, planes, ch, ny, nz, scale),
        out_shape=(
            jax.ShapeDtypeStruct((rows, nz), bf16),
            jax.ShapeDtypeStruct((rows, nz), bf16),
            jax.ShapeDtypeStruct((ch, 512), f32),
        ),
        in_specs=[smem, smem, vmem, vmem, vmem, vmem],
        out_specs=(vmem, vmem, vmem),
        scratch_shapes=[
            pltpu.VMEM((chunks, planes, ch, 128), bf16),
            pltpu.VMEM((n * planes, ch, 128), bf16),
            pltpu.VMEM((chunks * planes + 2, ch, 128), bf16),
            pltpu.VMEM((chunks, planes + 2, ch, 128), bf16),
            pltpu.VMEM((width + ch, cells), bf16),
            pltpu.VMEM((width, cells), bf16),
            pltpu.VMEM((planes + 2, ny, ch, nz), bf16),
            pltpu.VMEM((n, per, 128), f32),
            pltpu.VMEM((n, per, 128), f32),
            pltpu.VMEM((dps, per, 128), f32),
            pltpu.VMEM((n, per, 128), f32),
            pltpu.SemaphoreType.DMA((7,)),
            pltpu.SemaphoreType.DMA((7,)),
        ],
        compiler_params=pltpu.CompilerParams(
            collective_id=0, has_side_effects=True, vmem_limit_bytes=40 * 2**20
        ),
        cost_estimate=pl.CostEstimate(
            flops=6 * ch * width * cells, bytes_accessed=8 * rows * nz, transcendentals=2 * ch * cells
        ),
    )(
        offsets,
        flip_bits,
        features.reshape(rows, nz),
        weight.reshape(width, ch),
        conv_bias.reshape(ch, 1),
        cotangent.reshape(rows, nz),
    )
    grad_weight = grad_w[:, :width].reshape(ch, taps, ch).transpose(1, 0, 2)
    return (
        hidden.reshape(features.shape),
        grad_in.reshape(features.shape),
        grad_weight,
        grad_w[:, width],
    )


def solution(mesh):
    in_specs = (
        P("dp", None, "gx", None, None),
        P("dp", None),
        P("dp", None),
        P(),
        P(),
        P("dp", None, "gx", None, None),
    )
    out_specs = (P("dp", None, "gx", None, None), P("dp", None, "gx", None, None), P(), P())
    return jax.shard_map(
        on_device, mesh=mesh, in_specs=in_specs, out_specs=out_specs, check_vma=False
    )
```

```python
import functools
import math

import jax
import jax.numpy as jnp
from jax import lax
from jax.experimental import pallas as pl
from jax.experimental.pallas import tpu as pltpu
from jax.sharding import PartitionSpec as P

MESH = pl.DeviceIdType.MESH
bf16, f32 = jnp.bfloat16, jnp.float32


def iota(shape, dim):
    return lax.broadcasted_iota(jnp.int32, shape, dim)


def one_hot(mask):
    return jnp.where(mask, 1.0, 0.0).astype(bf16)


def mm(a, b):
    return jnp.dot(a, b, preferred_element_type=f32)


def mm_t(a, b):
    return lax.dot_general(a, b, (((1,), (1,)), ((), ())), preferred_element_type=f32)


def gelu_parts(pre_act):
    normal_cdf = 0.5 * (1.0 + lax.erf(pre_act * 0.7071067811865476))
    density = jnp.exp(-0.5 * pre_act * pre_act) * 0.3989422804014327
    return (pre_act * normal_cdf, normal_cdf + pre_act * density)


def wait_bytes(ref, sem):
    pltpu.make_async_copy(ref, ref, sem).wait()


def kernel(
    n, dps, planes, ch, ny, nz, scale,
    off_ref, flip_ref, feat_ref, weight_ref, bias_ref, cot_ref,
    hid_out, gin_out, gw_out,
    hid_ref, gin_ref, gw_ref, feat, weight, cot_in, send1, recv1, stag, recv2, cols, gcols, gext, rs, rsr, dpr, ag,
    load_sems, store_sems, send_sems, recv_sems,
):
    me, my_dp = lax.axis_index("gx"), lax.axis_index("dp")
    taps = 27
    rows = ch * planes * ny
    chunks = ny * nz // 128
    nx = n * planes
    per = rs.shape[1]

    loads = [
        pltpu.make_async_copy(source, target, load_sems.at[k])
        for k, (source, target) in enumerate(
            [(feat_ref, feat), (weight_ref, weight), (cot_ref, cot_in)]
        )
    ]
    for load in loads:
        load.start()
    stores = [
        pltpu.make_async_copy(source, target, store_sems.at[k])
        for k, (source, target) in enumerate(
            [(hid_ref, hid_out), (gin_ref, gin_out), (gw_ref, gw_out)]
        )
    ]

    barrier = pltpu.get_barrier_semaphore()

    def greet(k, _):
        pl.semaphore_signal(
            barrier, inc=1, device_id={"gx": lax.rem(me + k, n)}, device_id_type=MESH
        )
        return 0

    def greet_dp(k, _):
        pl.semaphore_signal(
            barrier, inc=1, device_id={"dp": lax.rem(my_dp + k, dps)}, device_id_type=MESH
        )
        return 0

    lax.fori_loop(1, n, greet, 0)
    lax.fori_loop(1, dps, greet_dp, 0)

    r_out = iota((rows, 1), 0)
    r_in = iota((1, rows), 1)
    out_c, out_y, out_x = r_out & (ch - 1), (r_out // ch) & (ny - 1), r_out // (ch * ny)
    base = (out_c * planes + out_x) * ny
    src_y = jnp.where(flip_ref[0, 1] == 1, ny - 1 - out_y, out_y) - off_ref[0, 1]
    order = one_hot(r_in == base + out_y)
    order_aug = one_hot(r_in == base + (src_y & (ny - 1)))
    zi, zo = iota((nz, 1), 0), iota((1, nz), 1)
    src_z = jnp.where(flip_ref[0, 2] == 1, nz - 1 - zo, zo) - off_ref[0, 2]
    perm_z = one_hot(zi == (src_z & (nz - 1)))
    loads[0].wait()
    local = mm(feat[...], perm_z).astype(bf16)
    local = mm(order_aug, local).astype(bf16)
    for j in range(chunks):
        y, half = j // 2, j % 2
        for x in range(planes):
            r0 = (x * ny + y) * ch
            send1[j, x] = local[r0 : r0 + ch, half * 128 : half * 128 + 128]

    pl.semaphore_wait(barrier, n + dps - 2)

    def start1(k, _):
        peer = lax.rem(me + k, n)
        pltpu.make_async_remote_copy(
            src_ref=send1.at[lax.rem(peer, chunks)],
            dst_ref=recv1.at[pl.ds(me * planes, planes)],
            send_sem=send_sems.at[0],
            recv_sem=recv_sems.at[0],
            device_id={"gx": peer},
            device_id_type=MESH,
        ).start()
        return 0

    lax.fori_loop(1, n, start1, 0)
    my_chunk = lax.rem(me, chunks)
    group = me // chunks * chunks
    recv1[pl.ds(me * planes, planes)] = send1[my_chunk]

    width = taps * ch
    loads[1].wait()
    tap_of = one_hot(iota((taps, 1), 0) == iota((1, width), 1) // ch)
    spread = mm(weight[...], tap_of)
    pair, lane_c = iota((ch * ch, 1), 0), iota((1, width), 1) & (ch - 1)
    by_in = jnp.where((pair & (ch - 1)) == lane_c, spread, 0.0).astype(bf16)
    by_out = jnp.where(pair // ch == lane_c, spread, 0.0).astype(bf16)
    row, across = iota((ch, 1), 0), iota((1, ch * ch), 1)
    w_fwd = mm(one_hot(row == across // ch), by_in).astype(bf16)
    w_bwd = mm(one_hot(row == (across & (ch - 1))), by_out).astype(bf16)
    bias = jnp.sum(
        jnp.where(iota((ch, 1), 0) == iota((1, ch), 1), bias_ref[...], 0.0), axis=1, keepdims=True
    )
    z_less = one_hot(zi == ((zo - 1) & (nz - 1)))
    z_more = one_hot(zi == ((zo + 1) & (nz - 1)))
    cols[width : width + ch] = jnp.ones((ch, cols.shape[1]), bf16)
    loads[2].wait()
    cot = mm(order, cot_in[...])

    wait_bytes(recv1.at[pl.ds(0, (n - 1) * planes)], recv_sems.at[0])

    def routed(p):
        target = lax.rem(group * planes + (p - 1 + nx), nx)
        source = jnp.where(flip_ref[0, 0] == 1, nx - 1 - target, target) - off_ref[0, 0]
        return recv1[lax.rem(source + nx, nx)]

    first, last = planes, planes + 1
    for q in range(chunks):
        for x in range(planes):
            plane = routed(q * planes + x + 1)
            stag[q, x] = plane
            if x == planes - 1:
                stag[(q + 1) % chunks, first] = plane
            if x == 0:
                stag[(q - 1) % chunks, last] = plane
    stag[0, first] = routed(0)
    stag[chunks - 1, last] = routed(chunks * planes + 1)

    def start2(begin, count, k, _):
        q = lax.rem(my_chunk + k, chunks)
        pltpu.make_async_remote_copy(
            src_ref=stag.at[q, pl.ds(begin, count)],
            dst_ref=recv2.at[my_chunk, pl.ds(begin, count)],
            send_sem=send_sems.at[1 if begin == 0 else 7],
            recv_sem=recv_sems.at[1 if begin == 0 else 7],
            device_id={"gx": group + q},
            device_id_type=MESH,
        ).start()
        return 0

    lax.fori_loop(1, chunks, functools.partial(start2, 0, planes), 0)
    lax.fori_loop(1, chunks, functools.partial(start2, planes, 2), 0)
    recv2[my_chunk] = stag[my_chunk]

    def lane(x, y):
        return (x * ny + y) * nz

    def columns(p):
        slot = first if p == 0 else last if p == planes + 1 else p - 1
        mid = [
            jnp.concatenate([recv2[2 * y, slot], recv2[2 * y + 1, slot]], axis=1)
            for y in range(ny)
        ]
        stacked = jnp.concatenate(mid, axis=0)
        shifts = [mm(stacked, z_less).astype(bf16), stacked, mm(stacked, z_more).astype(bf16)]
        for a in range(3):
            x = p - a
            if not 0 <= x < planes:
                continue
            for e in range(3):
                for h in range(3):
                    t = 9 * a + 3 * e + h
                    for y in range(ny):
                        s = (y + e - 1) % ny
                        cols[t * ch : t * ch + ch, lane(x, y) : lane(x, y) + nz] = shifts[h][
                            s * ch : s * ch + ch
                        ]

    wait_bytes(recv2.at[pl.ds(0, chunks - 1), pl.ds(0, planes)], recv_sems.at[1])
    for p in range(1, planes + 1):
        columns(p)
    wait_bytes(recv2.at[pl.ds(0, chunks - 1), pl.ds(planes, 2)], recv_sems.at[7])
    columns(0)
    columns(planes + 1)

    for x in range(planes):
        for y in range(ny):
            r0 = (x * ny + y) * ch
            at = slice(lane(x, y), lane(x, y) + nz)
            pre = mm(w_fwd, cols[0:width, at]) + bias
            act, slope = gelu_parts(pre)
            hid_ref[r0 : r0 + ch] = act.astype(bf16)
            gext[x + 1, y] = (cot[r0 : r0 + ch] * slope).astype(bf16)

    right, left = lax.rem(me + 1, n), lax.rem(me + n - 1, n)
    halos = [
        pltpu.make_async_remote_copy(
            src_ref=gext.at[here],
            dst_ref=gext.at[there],
            send_sem=send_sems.at[2 + side],
            recv_sem=recv_sems.at[2 + side],
            device_id={"gx": peer},
            device_id_type=MESH,
        )
        for side, (here, there, peer) in enumerate(
            [(planes, 0, right), (1, planes + 1, left)]
        )
    ]
    for halo in halos:
        halo.start()

    gw = jnp.zeros((ch, width + ch), f32)
    for x in range(planes):
        for y in range(ny):
            gw = gw + mm_t(gext[x + 1, y], cols[:, lane(x, y) : lane(x, y) + nz])
    gw = jnp.concatenate([gw, jnp.zeros((ch, 512 - width - ch), f32)], axis=1)
    groups = ch // per
    for k in range(n):
        g, q = k % groups, k // groups
        rs[k] = gw[g * per : g * per + per, q * 128 : q * 128 + 128]

    def start_rs(k, _):
        peer = lax.rem(me + k, n)
        pltpu.make_async_remote_copy(
            src_ref=rs.at[peer],
            dst_ref=rsr.at[me],
            send_sem=send_sems.at[4],
            recv_sem=recv_sems.at[4],
            device_id={"gx": peer},
            device_id_type=MESH,
        ).start()
        return 0

    lax.fori_loop(1, n, start_rs, 0)
    rsr[me] = rs[me]
    stores[0].start()

    def grad_columns(p):
        stacked = jnp.concatenate([gext[p, y] for y in range(ny)], axis=0)
        shifts = [mm(stacked, z_more).astype(bf16), stacked, mm(stacked, z_less).astype(bf16)]
        for a in range(3):
            x = p + a - 2
            if not 0 <= x < planes:
                continue
            for e in range(3):
                for h in range(3):
                    t = 9 * a + 3 * e + h
                    for y in range(ny):
                        s = (y + 1 - e) % ny
                        gcols[t * ch : t * ch + ch, lane(x, y) : lane(x, y) + nz] = shifts[h][
                            s * ch : s * ch + ch
                        ]

    for p in range(1, planes + 1):
        grad_columns(p)

    wait_bytes(rsr.at[pl.ds(0, n - 1)], recv_sems.at[4])
    total = rsr[0]
    for k in range(1, n):
        total = total + rsr[k]
    dpr[my_dp] = total

    def start_dp(k, _):
        pltpu.make_async_remote_copy(
            src_ref=dpr.at[my_dp],
            dst_ref=dpr.at[my_dp],
            send_sem=send_sems.at[5],
            recv_sem=recv_sems.at[5],
            device_id={"dp": lax.rem(my_dp + k, dps)},
            device_id_type=MESH,
        ).start()
        return 0

    lax.fori_loop(1, dps, start_dp, 0)

    for halo in halos:
        halo.wait()
    grad_columns(0)
    grad_columns(planes + 1)

    wait_bytes(dpr.at[pl.ds(0, dps - 1)], recv_sems.at[5])
    total = dpr[0]
    for k in range(1, dps):
        total = total + dpr[k]
    ag[me] = total * scale

    def start_ag(k, _):
        pltpu.make_async_remote_copy(
            src_ref=ag.at[me],
            dst_ref=ag.at[me],
            send_sem=send_sems.at[6],
            recv_sem=recv_sems.at[6],
            device_id={"gx": lax.rem(me + k, n)},
            device_id_type=MESH,
        ).start()
        return 0

    lax.fori_loop(1, n, start_ag, 0)

    for x in range(planes):
        for y in range(ny):
            r0 = (x * ny + y) * ch
            grad = mm(w_bwd, gcols[:, lane(x, y) : lane(x, y) + nz])
            gin_ref[r0 : r0 + ch] = grad.astype(bf16)

    stores[1].start()
    wait_bytes(ag.at[pl.ds(0, n - 1)], recv_sems.at[6])
    for k in range(n):
        g, q = k % groups, k // groups
        gw_ref[g * per : g * per + per, q * 128 : q * 128 + 128] = ag[k]

    stores[2].start()
    wait_bytes(recv1.at[pl.ds(0, (n - 1) * planes)], send_sems.at[0])
    wait_bytes(recv2.at[pl.ds(0, chunks - 1), pl.ds(0, planes)], send_sems.at[1])
    wait_bytes(recv2.at[pl.ds(0, chunks - 1), pl.ds(planes, 2)], send_sems.at[7])
    wait_bytes(rsr.at[pl.ds(0, n - 1)], send_sems.at[4])
    wait_bytes(dpr.at[pl.ds(0, dps - 1)], send_sems.at[5])
    wait_bytes(ag.at[pl.ds(0, n - 1)], send_sems.at[6])
    for store in stores:
        store.wait()


def finish(
    planes, ch, ny, nz, taps,
    hid_in, gin_in, gw_in,
    hid_out, gin_out, gw_out, gb_out,
    hid_ref, gin_ref, gw_ref, hid, gin, gw, gb, load_sems, sems,
):
    rows, width = ch * planes * ny, taps * ch
    loads = [
        pltpu.make_async_copy(source, target, load_sems.at[k])
        for k, (source, target) in enumerate(
            [(hid_in, hid_ref), (gin_in, gin_ref), (gw_in, gw_ref)]
        )
    ]
    for load in loads:
        load.start()
    stores = [
        pltpu.make_async_copy(source, target, sems.at[k])
        for k, (source, target) in enumerate(
            [(hid, hid_out), (gin, gin_out), (gw, gw_out), (gb, gb_out)]
        )
    ]
    r_in, r_out = iota((rows, 1), 0), iota((1, rows), 1)
    base = ((r_out & (ch - 1)) * planes + r_out // (ch * ny)) * ny
    order = one_hot(r_in == base + ((r_out // ch) & (ny - 1)))
    loads[0].wait()
    hid[...] = mm(order, hid_ref[...]).astype(bf16)
    stores[0].start()
    loads[1].wait()
    gin[...] = mm(order, gin_ref[...]).astype(bf16)
    stores[1].start()
    loads[2].wait()
    kept = (iota((ch, 1), 0)) == (iota((1, width), 1) & (ch - 1))
    pairs = jnp.concatenate(
        [jnp.where(kept, gw_ref[o : o + 1, 0:width], 0.0) for o in range(ch)], axis=0
    )
    tap_of = one_hot(iota((width, 1), 0) // ch == iota((1, taps), 1))
    high = pairs.astype(bf16)
    rest = pairs - high.astype(f32)
    mid = rest.astype(bf16)
    low = (rest - mid.astype(f32)).astype(bf16)
    gw[...] = mm(high, tap_of) + (mm(mid, tap_of) + mm(low, tap_of))
    stores[2].start()
    gb[...] = jnp.sum(
        jnp.where(iota((ch, 1), 0) == iota((1, ch), 1), gw_ref[:, width : width + 1], 0.0),
        axis=0, keepdims=True,
    )
    stores[3].start()
    for store in stores:
        store.wait()


def on_device(features, offsets, flip_bits, weight, conv_bias, cotangent):
    _, ch, planes, ny, nz = features.shape
    n, dps = lax.axis_size("gx"), lax.axis_size("dp")
    taps = weight.shape[0]
    rows, cells, chunks = ch * planes * ny, planes * ny * nz, ny * nz // 128
    width = taps * ch
    per = ch * 512 // (128 * n)
    scale = 1.0 / math.sqrt(dps * n * cells)
    vmem = pl.BlockSpec(memory_space=pltpu.VMEM)
    smem = pl.BlockSpec(memory_space=pltpu.SMEM)
    hbm = pl.BlockSpec(memory_space=pltpu.HBM)
    hidden, grad_in, grad_w = pl.pallas_call(
        functools.partial(kernel, n, dps, planes, ch, ny, nz, scale),
        out_shape=(
            jax.ShapeDtypeStruct((rows, nz), bf16),
            jax.ShapeDtypeStruct((rows, nz), bf16),
            jax.ShapeDtypeStruct((ch, 512), f32),
        ),
        in_specs=[smem, smem, hbm, hbm, vmem, hbm],
        out_specs=(hbm, hbm, hbm),
        scratch_shapes=[
            pltpu.VMEM((rows, nz), bf16),
            pltpu.VMEM((rows, nz), bf16),
            pltpu.VMEM((ch, 512), f32),
            pltpu.VMEM((rows, nz), bf16),
            pltpu.VMEM((ch * ch, taps), bf16),
            pltpu.VMEM((rows, nz), bf16),
            pltpu.VMEM((chunks, planes, ch, 128), bf16),
            pltpu.VMEM((n * planes, ch, 128), bf16),
            pltpu.VMEM((chunks, planes + 2, ch, 128), bf16),
            pltpu.VMEM((chunks, planes + 2, ch, 128), bf16),
            pltpu.VMEM((width + ch, cells), bf16),
            pltpu.VMEM((width, cells), bf16),
            pltpu.VMEM((planes + 2, ny, ch, nz), bf16),
            pltpu.VMEM((n, per, 128), f32),
            pltpu.VMEM((n, per, 128), f32),
            pltpu.VMEM((dps, per, 128), f32),
            pltpu.VMEM((n, per, 128), f32),
            pltpu.SemaphoreType.DMA((3,)),
            pltpu.SemaphoreType.DMA((3,)),
            pltpu.SemaphoreType.DMA((8,)),
            pltpu.SemaphoreType.DMA((8,)),
        ],
        compiler_params=pltpu.CompilerParams(
            collective_id=0, has_side_effects=True, vmem_limit_bytes=63 * 2**20
        ),
        cost_estimate=pl.CostEstimate(
            flops=6 * ch * width * cells, bytes_accessed=8 * rows * nz, transcendentals=2 * ch * cells
        ),
    )(
        offsets,
        flip_bits,
        features.reshape(rows, nz),
        weight.transpose(1, 2, 0).reshape(ch * ch, taps),
        conv_bias.reshape(1, ch),
        cotangent.reshape(rows, nz),
    )
    hidden, grad_in, grad_w, grad_b = pl.pallas_call(
        functools.partial(finish, planes, ch, ny, nz, taps),
        out_shape=(
            jax.ShapeDtypeStruct((rows, nz), bf16),
            jax.ShapeDtypeStruct((rows, nz), bf16),
            jax.ShapeDtypeStruct((ch * ch, taps), f32),
            jax.ShapeDtypeStruct((1, ch), f32),
        ),
        in_specs=[hbm, hbm, hbm],
        out_specs=(hbm, hbm, hbm, hbm),
        scratch_shapes=[
            pltpu.VMEM((rows, nz), bf16),
            pltpu.VMEM((rows, nz), bf16),
            pltpu.VMEM((ch, 512), f32),
            pltpu.VMEM((rows, nz), bf16),
            pltpu.VMEM((rows, nz), bf16),
            pltpu.VMEM((ch * ch, taps), f32),
            pltpu.VMEM((1, ch), f32),
            pltpu.SemaphoreType.DMA((3,)),
            pltpu.SemaphoreType.DMA((4,)),
        ],
        compiler_params=pltpu.CompilerParams(vmem_limit_bytes=63 * 2**20),
    )(hidden, grad_in, grad_w)
    return (
        hidden.reshape(features.shape),
        grad_in.reshape(features.shape),
        grad_w.reshape(ch, ch, taps).transpose(2, 0, 1),
        grad_b.reshape(ch),
    )


def solution(mesh):
    in_specs = (
        P("dp", None, "gx", None, None),
        P("dp", None),
        P("dp", None),
        P(),
        P(),
        P("dp", None, "gx", None, None),
    )
    out_specs = (P("dp", None, "gx", None, None), P("dp", None, "gx", None, None), P(), P())
    return jax.shard_map(
        on_device, mesh=mesh, in_specs=in_specs, out_specs=out_specs, check_vma=False
    )
```

```python
import functools
import math

import jax
import jax.numpy as jnp
from jax import lax
from jax.experimental import pallas as pl
from jax.experimental.pallas import tpu as pltpu
from jax.sharding import PartitionSpec as P

MESH = pl.DeviceIdType.MESH
bf16, f32 = jnp.bfloat16, jnp.float32


def iota(shape, dim):
    return lax.broadcasted_iota(jnp.int32, shape, dim)


def one_hot(mask):
    return jnp.where(mask, 1.0, 0.0).astype(bf16)


def mm(a, b):
    return jnp.dot(a, b, preferred_element_type=f32)


def mm_t(a, b):
    return lax.dot_general(a, b, (((1,), (1,)), ((), ())), preferred_element_type=f32)


def gelu_parts(pre_act):
    normal_cdf = 0.5 * (1.0 + lax.erf(pre_act * 0.7071067811865476))
    density = jnp.exp(-0.5 * pre_act * pre_act) * 0.3989422804014327
    return (pre_act * normal_cdf, normal_cdf + pre_act * density)


def wrap(index, count):
    if count & (count - 1) == 0:
        return index & (count - 1)
    return lax.rem(index + count, count)


def each_peer(count, body):
    lax.fori_loop(1, count, lambda k, _: body(k) or 0, 0, unroll=count <= 16)


def wait_bytes(ref, sem):
    pltpu.make_async_copy(ref, ref, sem).wait()


def kernel(
    n, dps, planes, ch, ny, nz, scale,
    off_ref, flip_ref, feat_ref, weight_ref, bias_ref, cot_ref,
    hid_out, gin_out, gw_out,
    hid_ref, gin_ref, gw_ref, feat, weight, cot_in, send1, recv1, stag, recv2, cols, gcols, gext, rs, rsr, dpr, ag,
    load_sems, store_sems, send_sems, recv_sems,
):
    me, my_dp = lax.axis_index("gx"), lax.axis_index("dp")
    taps = 27
    rows = ch * planes * ny
    chunks = ny * nz // 128
    nx = n * planes
    per = rs.shape[1]

    loads = [
        pltpu.make_async_copy(source, target, load_sems.at[k])
        for k, (source, target) in enumerate(
            [(feat_ref, feat), (weight_ref, weight), (cot_ref, cot_in)]
        )
    ]
    for load in loads:
        load.start()
    stores = [
        pltpu.make_async_copy(source, target, store_sems.at[k])
        for k, (source, target) in enumerate(
            [(hid_ref, hid_out), (gin_ref, gin_out), (gw_ref, gw_out)]
        )
    ]

    barrier = pltpu.get_barrier_semaphore()

    def greet(k):
        pl.semaphore_signal(
            barrier, inc=1, device_id={"gx": wrap(me + k, n)}, device_id_type=MESH
        )

    def greet_dp(k):
        pl.semaphore_signal(
            barrier, inc=1, device_id={"dp": wrap(my_dp + k, dps)}, device_id_type=MESH
        )

    each_peer(n, greet)
    each_peer(dps, greet_dp)

    r_out = iota((rows, 1), 0)
    r_in = iota((1, rows), 1)
    out_c, out_y, out_x = r_out & (ch - 1), (r_out // ch) & (ny - 1), r_out // (ch * ny)
    base = (out_c * planes + out_x) * ny
    src_y = jnp.where(flip_ref[0, 1] == 1, ny - 1 - out_y, out_y) - off_ref[0, 1]
    order = one_hot(r_in == base + out_y)
    order_aug = one_hot(r_in == base + (src_y & (ny - 1)))
    zi, zo = iota((nz, 1), 0), iota((1, nz), 1)
    src_z = jnp.where(flip_ref[0, 2] == 1, nz - 1 - zo, zo) - off_ref[0, 2]
    perm_z = one_hot(zi == (src_z & (nz - 1)))
    loads[0].wait()
    local = mm(feat[...], perm_z).astype(bf16)
    local = mm(order_aug, local).astype(bf16)
    for j in range(chunks):
        y, half = j // 2, j % 2
        for x in range(planes):
            r0 = (x * ny + y) * ch
            send1[j, x] = local[r0 : r0 + ch, half * 128 : half * 128 + 128]

    pl.semaphore_wait(barrier, n + dps - 2)

    def start1(k):
        peer = wrap(me + k, n)
        pltpu.make_async_remote_copy(
            src_ref=send1.at[wrap(peer, chunks)],
            dst_ref=recv1.at[pl.ds(me * planes, planes)],
            send_sem=send_sems.at[0],
            recv_sem=recv_sems.at[0],
            device_id={"gx": peer},
            device_id_type=MESH,
        ).start()

    each_peer(n, start1)
    my_chunk = wrap(me, chunks)
    group = me // chunks * chunks
    recv1[pl.ds(me * planes, planes)] = send1[my_chunk]

    width = taps * ch
    loads[1].wait()
    tap_of = one_hot(iota((taps, 1), 0) == iota((1, width), 1) // ch)
    spread = mm(weight[...], tap_of)
    pair, lane_c = iota((ch * ch, 1), 0), iota((1, width), 1) & (ch - 1)
    by_in = jnp.where((pair & (ch - 1)) == lane_c, spread, 0.0).astype(bf16)
    by_out = jnp.where(pair // ch == lane_c, spread, 0.0).astype(bf16)
    row, across = iota((ch, 1), 0), iota((1, ch * ch), 1)
    w_fwd = mm(one_hot(row == across // ch), by_in).astype(bf16)
    w_bwd = mm(one_hot(row == (across & (ch - 1))), by_out).astype(bf16)
    bias = jnp.sum(
        jnp.where(iota((ch, 1), 0) == iota((1, ch), 1), bias_ref[...], 0.0), axis=1, keepdims=True
    )
    z_less = one_hot(zi == ((zo - 1) & (nz - 1)))
    z_more = one_hot(zi == ((zo + 1) & (nz - 1)))
    cols[width : width + ch] = jnp.ones((ch, cols.shape[1]), bf16)
    loads[2].wait()
    cot = mm(order, cot_in[...])

    sources = []
    for p in range(chunks * planes + 2):
        target = wrap(group * planes + (p - 1), nx)
        source = jnp.where(flip_ref[0, 0] == 1, nx - 1 - target, target) - off_ref[0, 0]
        sources.append(wrap(source, nx))

    wait_bytes(recv1.at[pl.ds(0, (n - 1) * planes)], recv_sems.at[0])

    def routed(p):
        return recv1[sources[p]]

    first, last = planes, planes + 1
    for q in range(chunks):
        for x in range(planes):
            plane = routed(q * planes + x + 1)
            stag[q, x] = plane
            if x == planes - 1:
                stag[(q + 1) % chunks, first] = plane
            if x == 0:
                stag[(q - 1) % chunks, last] = plane
    stag[0, first] = routed(0)
    stag[chunks - 1, last] = routed(chunks * planes + 1)

    def start2(begin, count, k):
        q = wrap(my_chunk + k, chunks)
        pltpu.make_async_remote_copy(
            src_ref=stag.at[q, pl.ds(begin, count)],
            dst_ref=recv2.at[my_chunk, pl.ds(begin, count)],
            send_sem=send_sems.at[1 if begin == 0 else 7],
            recv_sem=recv_sems.at[1 if begin == 0 else 7],
            device_id={"gx": group + q},
            device_id_type=MESH,
        ).start()

    each_peer(chunks, functools.partial(start2, 0, planes))
    each_peer(chunks, functools.partial(start2, planes, 2))
    recv2[my_chunk] = stag[my_chunk]

    def lane(x, y):
        return (x * ny + y) * nz

    def columns(p):
        slot = first if p == 0 else last if p == planes + 1 else p - 1
        mid = [
            jnp.concatenate([recv2[2 * y, slot], recv2[2 * y + 1, slot]], axis=1)
            for y in range(ny)
        ]
        stacked = jnp.concatenate(mid, axis=0)
        shifts = [mm(stacked, z_less).astype(bf16), stacked, mm(stacked, z_more).astype(bf16)]
        for a in range(3):
            x = p - a
            if not 0 <= x < planes:
                continue
            for e in range(3):
                for h in range(3):
                    t = 9 * a + 3 * e + h
                    for y in range(ny):
                        s = (y + e - 1) % ny
                        cols[t * ch : t * ch + ch, lane(x, y) : lane(x, y) + nz] = shifts[h][
                            s * ch : s * ch + ch
                        ]

    wait_bytes(recv2.at[pl.ds(0, chunks - 1), pl.ds(0, planes)], recv_sems.at[1])
    for p in range(1, planes + 1):
        columns(p)
    wait_bytes(recv2.at[pl.ds(0, chunks - 1), pl.ds(planes, 2)], recv_sems.at[7])
    columns(0)
    columns(planes + 1)

    hidden, gw = [], jnp.zeros((width + ch, ch), f32)
    for x in range(planes):
        grads = []
        for y in range(ny):
            r0 = (x * ny + y) * ch
            at = slice(lane(x, y), lane(x, y) + nz)
            pre = mm(w_fwd, cols[0:width, at]) + bias
            act, slope = gelu_parts(pre)
            hidden.append(act.astype(bf16))
            grads.append((cot[r0 : r0 + ch] * slope).astype(bf16))
            gext[x + 1, y] = grads[-1]
        gw = gw + mm_t(cols[:, lane(x, 0) : lane(x, 0) + ny * nz], jnp.concatenate(grads, axis=1))

    right, left = lax.rem(me + 1, n), lax.rem(me + n - 1, n)
    halos = [
        pltpu.make_async_remote_copy(
            src_ref=gext.at[here],
            dst_ref=gext.at[there],
            send_sem=send_sems.at[2 + side],
            recv_sem=recv_sems.at[2 + side],
            device_id={"gx": peer},
            device_id_type=MESH,
        )
        for side, (here, there, peer) in enumerate(
            [(planes, 0, right), (1, planes + 1, left)]
        )
    ]
    for halo in halos:
        halo.start()

    gw = jnp.concatenate([gw, jnp.zeros((512 - width - ch, ch), f32)], axis=0).T
    groups = ch // per
    for k in range(n):
        g, q = k % groups, k // groups
        rs[k] = gw[g * per : g * per + per, q * 128 : q * 128 + 128]

    def start_rs(k):
        peer = wrap(me + k, n)
        pltpu.make_async_remote_copy(
            src_ref=rs.at[peer],
            dst_ref=rsr.at[me],
            send_sem=send_sems.at[4],
            recv_sem=recv_sems.at[4],
            device_id={"gx": peer},
            device_id_type=MESH,
        ).start()

    each_peer(n, start_rs)
    rsr[me] = rs[me]

    b_out, b_in = iota((rows, 1), 0), iota((1, rows), 1)
    b_base = ((b_in & (ch - 1)) * planes + b_in // (ch * ny)) * ny
    back = one_hot(b_out == b_base + ((b_in // ch) & (ny - 1)))
    hid_ref[...] = mm(back, jnp.concatenate(hidden, axis=0)).astype(bf16)
    stores[0].start()

    def grad_columns(p):
        stacked = jnp.concatenate([gext[p, y] for y in range(ny)], axis=0)
        shifts = [mm(stacked, z_more).astype(bf16), stacked, mm(stacked, z_less).astype(bf16)]
        for a in range(3):
            x = p + a - 2
            if not 0 <= x < planes:
                continue
            for e in range(3):
                for h in range(3):
                    t = 9 * a + 3 * e + h
                    for y in range(ny):
                        s = (y + 1 - e) % ny
                        gcols[t * ch : t * ch + ch, lane(x, y) : lane(x, y) + nz] = shifts[h][
                            s * ch : s * ch + ch
                        ]

    for p in range(1, planes + 1):
        grad_columns(p)

    wait_bytes(rsr.at[pl.ds(0, n - 1)], recv_sems.at[4])
    total = rsr[0]
    for k in range(1, n):
        total = total + rsr[k]
    dpr[my_dp] = total

    def start_dp(k):
        pltpu.make_async_remote_copy(
            src_ref=dpr.at[my_dp],
            dst_ref=dpr.at[my_dp],
            send_sem=send_sems.at[5],
            recv_sem=recv_sems.at[5],
            device_id={"dp": wrap(my_dp + k, dps)},
            device_id_type=MESH,
        ).start()

    each_peer(dps, start_dp)

    for halo in halos:
        halo.wait()
    grad_columns(0)
    grad_columns(planes + 1)

    wait_bytes(dpr.at[pl.ds(0, dps - 1)], recv_sems.at[5])
    total = dpr[0]
    for k in range(1, dps):
        total = total + dpr[k]
    ag[me] = total * scale

    def start_ag(k):
        pltpu.make_async_remote_copy(
            src_ref=ag.at[me],
            dst_ref=ag.at[me],
            send_sem=send_sems.at[6],
            recv_sem=recv_sems.at[6],
            device_id={"gx": wrap(me + k, n)},
            device_id_type=MESH,
        ).start()

    each_peer(n, start_ag)

    grad_in = [
        mm(w_bwd, gcols[:, lane(x, y) : lane(x, y) + nz]).astype(bf16)
        for x in range(planes)
        for y in range(ny)
    ]
    gin_ref[...] = mm(back, jnp.concatenate(grad_in, axis=0)).astype(bf16)

    stores[1].start()
    wait_bytes(ag.at[pl.ds(0, n - 1)], recv_sems.at[6])
    for k in range(n):
        g, q = k % groups, k // groups
        gw_ref[g * per : g * per + per, q * 128 : q * 128 + 128] = ag[k]

    stores[2].start()
    wait_bytes(recv1.at[pl.ds(0, (n - 1) * planes)], send_sems.at[0])
    wait_bytes(recv2.at[pl.ds(0, chunks - 1), pl.ds(0, planes)], send_sems.at[1])
    wait_bytes(recv2.at[pl.ds(0, chunks - 1), pl.ds(planes, 2)], send_sems.at[7])
    wait_bytes(rsr.at[pl.ds(0, n - 1)], send_sems.at[4])
    wait_bytes(dpr.at[pl.ds(0, dps - 1)], send_sems.at[5])
    wait_bytes(ag.at[pl.ds(0, n - 1)], send_sems.at[6])
    for store in stores:
        store.wait()


def finish(
    ch, taps, hid_in, gin_in, gw_in, hid_out, gin_out, gw_out, gb_out, gw_ref, gw, gb, load_sem, sems
):
    width = taps * ch
    load = pltpu.make_async_copy(gw_in, gw_ref, load_sem)
    load.start()
    stores = [
        pltpu.make_async_copy(source, target, sems.at[k])
        for k, (source, target) in enumerate(
            [(hid_in, hid_out), (gin_in, gin_out), (gw, gw_out), (gb, gb_out)]
        )
    ]
    stores[0].start()
    stores[1].start()
    kept = iota((ch, 1), 0) == (iota((1, width), 1) & (ch - 1))
    tap_of = one_hot(iota((width, 1), 0) // ch == iota((1, taps), 1))
    load.wait()
    pairs = jnp.concatenate(
        [jnp.where(kept, gw_ref[o : o + 1, 0:width], 0.0) for o in range(ch)], axis=0
    )
    high = pairs.astype(bf16)
    rest = pairs - high.astype(f32)
    mid = rest.astype(bf16)
    low = (rest - mid.astype(f32)).astype(bf16)
    gw[...] = mm(high, tap_of) + (mm(mid, tap_of) + mm(low, tap_of))
    stores[2].start()
    gb[...] = jnp.sum(
        jnp.where(iota((ch, 1), 0) == iota((1, ch), 1), gw_ref[:, width : width + 1], 0.0),
        axis=0, keepdims=True,
    )
    stores[3].start()
    for store in stores:
        store.wait()


def on_device(features, offsets, flip_bits, weight, conv_bias, cotangent):
    _, ch, planes, ny, nz = features.shape
    n, dps = lax.axis_size("gx"), lax.axis_size("dp")
    taps = weight.shape[0]
    rows, cells, chunks = ch * planes * ny, planes * ny * nz, ny * nz // 128
    width = taps * ch
    per = ch * 512 // (128 * n)
    scale = 1.0 / math.sqrt(dps * n * cells)
    vmem = pl.BlockSpec(memory_space=pltpu.VMEM)
    smem = pl.BlockSpec(memory_space=pltpu.SMEM)
    hbm = pl.BlockSpec(memory_space=pltpu.HBM)
    hidden, grad_in, grad_w = pl.pallas_call(
        functools.partial(kernel, n, dps, planes, ch, ny, nz, scale),
        out_shape=(
            jax.ShapeDtypeStruct((rows, nz), bf16),
            jax.ShapeDtypeStruct((rows, nz), bf16),
            jax.ShapeDtypeStruct((ch, 512), f32),
        ),
        in_specs=[smem, smem, hbm, hbm, vmem, hbm],
        out_specs=(hbm, hbm, hbm),
        scratch_shapes=[
            pltpu.VMEM((rows, nz), bf16),
            pltpu.VMEM((rows, nz), bf16),
            pltpu.VMEM((ch, 512), f32),
            pltpu.VMEM((rows, nz), bf16),
            pltpu.VMEM((ch * ch, taps), bf16),
            pltpu.VMEM((rows, nz), bf16),
            pltpu.VMEM((chunks, planes, ch, 128), bf16),
            pltpu.VMEM((n * planes, ch, 128), bf16),
            pltpu.VMEM((chunks, planes + 2, ch, 128), bf16),
            pltpu.VMEM((chunks, planes + 2, ch, 128), bf16),
            pltpu.VMEM((width + ch, cells), bf16),
            pltpu.VMEM((width, cells), bf16),
            pltpu.VMEM((planes + 2, ny, ch, nz), bf16),
            pltpu.VMEM((n, per, 128), f32),
            pltpu.VMEM((n, per, 128), f32),
            pltpu.VMEM((dps, per, 128), f32),
            pltpu.VMEM((n, per, 128), f32),
            pltpu.SemaphoreType.DMA((3,)),
            pltpu.SemaphoreType.DMA((3,)),
            pltpu.SemaphoreType.DMA((8,)),
            pltpu.SemaphoreType.DMA((8,)),
        ],
        compiler_params=pltpu.CompilerParams(
            collective_id=0, has_side_effects=True, vmem_limit_bytes=63 * 2**20
        ),
        cost_estimate=pl.CostEstimate(
            flops=6 * ch * width * cells, bytes_accessed=8 * rows * nz, transcendentals=2 * ch * cells
        ),
    )(
        offsets,
        flip_bits,
        features.reshape(rows, nz),
        weight.transpose(1, 2, 0).reshape(ch * ch, taps),
        conv_bias.reshape(1, ch),
        cotangent.reshape(rows, nz),
    )
    hidden, grad_in, grad_w, grad_b = pl.pallas_call(
        functools.partial(finish, ch, taps),
        out_shape=(
            jax.ShapeDtypeStruct((rows, nz), bf16),
            jax.ShapeDtypeStruct((rows, nz), bf16),
            jax.ShapeDtypeStruct((ch * ch, taps), f32),
            jax.ShapeDtypeStruct((1, ch), f32),
        ),
        in_specs=[hbm, hbm, hbm],
        out_specs=(hbm, hbm, hbm, hbm),
        scratch_shapes=[
            pltpu.VMEM((ch, 512), f32),
            pltpu.VMEM((ch * ch, taps), f32),
            pltpu.VMEM((1, ch), f32),
            pltpu.SemaphoreType.DMA,
            pltpu.SemaphoreType.DMA((4,)),
        ],
        compiler_params=pltpu.CompilerParams(vmem_limit_bytes=63 * 2**20),
    )(hidden, grad_in, grad_w)
    return (
        hidden.reshape(features.shape),
        grad_in.reshape(features.shape),
        grad_w.reshape(ch, ch, taps).transpose(2, 0, 1),
        grad_b.reshape(ch),
    )


def solution(mesh):
    in_specs = (
        P("dp", None, "gx", None, None),
        P("dp", None),
        P("dp", None),
        P(),
        P(),
        P("dp", None, "gx", None, None),
    )
    out_specs = (P("dp", None, "gx", None, None), P("dp", None, "gx", None, None), P(), P())
    return jax.shard_map(
        on_device, mesh=mesh, in_specs=in_specs, out_specs=out_specs, check_vma=False
    )
```

```python
import functools
import math

import jax
import jax.numpy as jnp
from jax import lax
from jax.experimental import pallas as pl
from jax.experimental.pallas import tpu as pltpu
from jax.sharding import PartitionSpec as P

MESH = pl.DeviceIdType.MESH
bf16, f32 = jnp.bfloat16, jnp.float32


def iota(shape, dim):
    return lax.broadcasted_iota(jnp.int32, shape, dim)


def one_hot(mask):
    return jnp.where(mask, 1.0, 0.0).astype(bf16)


def mm(a, b):
    return jnp.dot(a, b, preferred_element_type=f32)


def mm_t(a, b):
    return lax.dot_general(a, b, (((1,), (1,)), ((), ())), preferred_element_type=f32)


def gelu_parts(pre_act):
    normal_cdf = 0.5 * (1.0 + lax.erf(pre_act * 0.7071067811865476))
    density = jnp.exp(-0.5 * pre_act * pre_act) * 0.3989422804014327
    return (pre_act * normal_cdf, normal_cdf + pre_act * density)


def wrap(index, count):
    if count & (count - 1) == 0:
        return index & (count - 1)
    return lax.rem(index + count, count)


def each_peer(count, body):
    lax.fori_loop(1, count, lambda k, _: body(k) or 0, 0, unroll=count <= 16)


def wait_bytes(ref, sem):
    pltpu.make_async_copy(ref, ref, sem).wait()


def kernel(
    n, dps, planes, ch, ny, nz, scale,
    off_ref, flip_ref, feat_ref, weight_ref, bias_ref, cot_ref,
    hid_out, gin_out, gw_out,
    hid_ref, gin_ref, gw_ref, feat, weight, cot_in, send1, recv1, stag, recv2, cols, gcols, gext, rs, rsr, dpr, ag,
    load_sems, store_sems, send_sems, recv_sems,
):
    me, my_dp = lax.axis_index("gx"), lax.axis_index("dp")
    taps = 27
    rows = ch * planes * ny
    chunks = ny * nz // 128
    nx = n * planes
    per = rs.shape[1]

    loads = [
        pltpu.make_async_copy(source, target, load_sems.at[k])
        for k, (source, target) in enumerate(
            [(feat_ref, feat), (weight_ref, weight), (cot_ref, cot_in)]
        )
    ]
    for load in loads:
        load.start()
    stores = [
        pltpu.make_async_copy(source, target, store_sems.at[k])
        for k, (source, target) in enumerate(
            [(hid_ref, hid_out), (gin_ref, gin_out), (gw_ref, gw_out)]
        )
    ]

    barrier = pltpu.get_barrier_semaphore()

    def greet(k):
        pl.semaphore_signal(
            barrier, inc=1, device_id={"gx": wrap(me + k, n)}, device_id_type=MESH
        )

    def greet_dp(k):
        pl.semaphore_signal(
            barrier, inc=1, device_id={"dp": wrap(my_dp + k, dps)}, device_id_type=MESH
        )

    each_peer(n, greet)
    each_peer(dps, greet_dp)

    r_out = iota((rows, 1), 0)
    r_in = iota((1, rows), 1)
    out_c, out_y, out_x = r_out & (ch - 1), (r_out // ch) & (ny - 1), r_out // (ch * ny)
    base = (out_c * planes + out_x) * ny
    src_y = jnp.where(flip_ref[0, 1] == 1, ny - 1 - out_y, out_y) - off_ref[0, 1]
    order = one_hot(r_in == base + out_y)
    order_aug = one_hot(r_in == base + (src_y & (ny - 1)))
    zi, zo = iota((nz, 1), 0), iota((1, nz), 1)
    src_z = jnp.where(flip_ref[0, 2] == 1, nz - 1 - zo, zo) - off_ref[0, 2]
    perm_z = one_hot(zi == (src_z & (nz - 1)))
    loads[0].wait()
    local = mm(feat[...], perm_z).astype(bf16)
    local = mm(order_aug, local).astype(bf16)
    for j in range(chunks):
        y, half = j // 2, j % 2
        for x in range(planes):
            r0 = (x * ny + y) * ch
            send1[j, x] = local[r0 : r0 + ch, half * 128 : half * 128 + 128]

    pl.semaphore_wait(barrier, n + dps - 2)

    def start1(k):
        peer = wrap(me + k, n)
        pltpu.make_async_remote_copy(
            src_ref=send1.at[wrap(peer, chunks)],
            dst_ref=recv1.at[pl.ds(me * planes, planes)],
            send_sem=send_sems.at[0],
            recv_sem=recv_sems.at[0],
            device_id={"gx": peer},
            device_id_type=MESH,
        ).start()

    each_peer(n, start1)
    my_chunk = wrap(me, chunks)
    group = me // chunks * chunks
    recv1[pl.ds(me * planes, planes)] = send1[my_chunk]

    width = taps * ch
    loads[1].wait()
    tap_of = one_hot(iota((taps, 1), 0) == iota((1, width), 1) // ch)
    spread = mm(weight[...], tap_of)
    pair, lane_c = iota((ch * ch, 1), 0), iota((1, width), 1) & (ch - 1)
    by_in = jnp.where((pair & (ch - 1)) == lane_c, spread, 0.0).astype(bf16)
    by_out = jnp.where(pair // ch == lane_c, spread, 0.0).astype(bf16)
    row, across = iota((ch, 1), 0), iota((1, ch * ch), 1)
    w_fwd = mm(one_hot(row == across // ch), by_in).astype(bf16)
    w_bwd = mm(one_hot(row == (across & (ch - 1))), by_out).astype(bf16)
    bias = jnp.sum(
        jnp.where(iota((ch, 1), 0) == iota((1, ch), 1), bias_ref[...], 0.0), axis=1, keepdims=True
    )
    z_less = one_hot(zi == ((zo - 1) & (nz - 1)))
    z_more = one_hot(zi == ((zo + 1) & (nz - 1)))
    cols[width : width + ch] = jnp.ones((ch, cols.shape[1]), bf16)
    loads[2].wait()
    cot = mm(order, cot_in[...])

    sources = []
    for p in range(chunks * planes + 2):
        target = wrap(group * planes + (p - 1), nx)
        source = jnp.where(flip_ref[0, 0] == 1, nx - 1 - target, target) - off_ref[0, 0]
        sources.append(wrap(source, nx))

    wait_bytes(recv1.at[pl.ds(0, (n - 1) * planes)], recv_sems.at[0])

    def routed(p):
        return recv1[sources[p]]

    first, last = planes, planes + 1
    for q in range(chunks):
        for x in range(planes):
            plane = routed(q * planes + x + 1)
            stag[q, x] = plane
            if x == planes - 1:
                stag[(q + 1) % chunks, first] = plane
            if x == 0:
                stag[(q - 1) % chunks, last] = plane
    stag[0, first] = routed(0)
    stag[chunks - 1, last] = routed(chunks * planes + 1)

    def start2(begin, count, k):
        q = wrap(my_chunk + k, chunks)
        pltpu.make_async_remote_copy(
            src_ref=stag.at[q, pl.ds(begin, count)],
            dst_ref=recv2.at[my_chunk, pl.ds(begin, count)],
            send_sem=send_sems.at[1 if begin == 0 else 7],
            recv_sem=recv_sems.at[1 if begin == 0 else 7],
            device_id={"gx": group + q},
            device_id_type=MESH,
        ).start()

    each_peer(chunks, functools.partial(start2, 0, planes))
    each_peer(chunks, functools.partial(start2, planes, 2))
    recv2[my_chunk] = stag[my_chunk]

    def lane(x, y):
        return (x * ny + y) * nz

    def columns(p):
        slot = first if p == 0 else last if p == planes + 1 else p - 1
        mid = [
            jnp.concatenate([recv2[2 * y, slot], recv2[2 * y + 1, slot]], axis=1)
            for y in range(ny)
        ]
        stacked = jnp.concatenate(mid, axis=0)
        shifts = [mm(stacked, z_less).astype(bf16), stacked, mm(stacked, z_more).astype(bf16)]
        for a in range(3):
            x = p - a
            if not 0 <= x < planes:
                continue
            for e in range(3):
                for h in range(3):
                    t = 9 * a + 3 * e + h
                    for y in range(ny):
                        s = (y + e - 1) % ny
                        cols[t * ch : t * ch + ch, lane(x, y) : lane(x, y) + nz] = shifts[h][
                            s * ch : s * ch + ch
                        ]

    wait_bytes(recv2.at[pl.ds(0, chunks - 1), pl.ds(0, planes)], recv_sems.at[1])
    for p in range(1, planes + 1):
        columns(p)
    wait_bytes(recv2.at[pl.ds(0, chunks - 1), pl.ds(planes, 2)], recv_sems.at[7])
    columns(0)
    columns(planes + 1)

    hidden = []
    for x in range(planes):
        for y in range(ny):
            r0 = (x * ny + y) * ch
            at = slice(lane(x, y), lane(x, y) + nz)
            pre = mm(w_fwd, cols[0:width, at]) + bias
            act, slope = gelu_parts(pre)
            hidden.append(act.astype(bf16))
            gext[x + 1, y] = (cot[r0 : r0 + ch] * slope).astype(bf16)

    right, left = lax.rem(me + 1, n), lax.rem(me + n - 1, n)
    halos = [
        pltpu.make_async_remote_copy(
            src_ref=gext.at[here],
            dst_ref=gext.at[there],
            send_sem=send_sems.at[2 + side],
            recv_sem=recv_sems.at[2 + side],
            device_id={"gx": peer},
            device_id_type=MESH,
        )
        for side, (here, there, peer) in enumerate(
            [(planes, 0, right), (1, planes + 1, left)]
        )
    ]
    gw = jnp.zeros((ch, width + ch), f32)
    for x in range(planes):
        for y in range(ny):
            gw = gw + mm_t(gext[x + 1, y], cols[:, lane(x, y) : lane(x, y) + nz])
    gw = jnp.concatenate([gw, jnp.zeros((ch, 512 - width - ch), f32)], axis=1)
    groups = ch // per
    for k in range(n):
        g, q = k % groups, k // groups
        rs[k] = gw[g * per : g * per + per, q * 128 : q * 128 + 128]

    def start_rs(k):
        peer = wrap(me + k, n)
        pltpu.make_async_remote_copy(
            src_ref=rs.at[peer],
            dst_ref=rsr.at[me],
            send_sem=send_sems.at[4],
            recv_sem=recv_sems.at[4],
            device_id={"gx": peer},
            device_id_type=MESH,
        ).start()

    each_peer(n, start_rs)
    rsr[me] = rs[me]
    for halo in halos:
        halo.start()

    b_out, b_in = iota((rows, 1), 0), iota((1, rows), 1)
    b_base = ((b_in & (ch - 1)) * planes + b_in // (ch * ny)) * ny
    back = one_hot(b_out == b_base + ((b_in // ch) & (ny - 1)))
    hid_ref[...] = mm(back, jnp.concatenate(hidden, axis=0)).astype(bf16)
    stores[0].start()

    def grad_columns(p):
        stacked = jnp.concatenate([gext[p, y] for y in range(ny)], axis=0)
        shifts = [mm(stacked, z_more).astype(bf16), stacked, mm(stacked, z_less).astype(bf16)]
        for a in range(3):
            x = p + a - 2
            if not 0 <= x < planes:
                continue
            for e in range(3):
                for h in range(3):
                    t = 9 * a + 3 * e + h
                    for y in range(ny):
                        s = (y + 1 - e) % ny
                        gcols[t * ch : t * ch + ch, lane(x, y) : lane(x, y) + nz] = shifts[h][
                            s * ch : s * ch + ch
                        ]

    for p in range(1, planes + 1):
        grad_columns(p)

    wait_bytes(rsr.at[pl.ds(0, n - 1)], recv_sems.at[4])
    total = rsr[0]
    for k in range(1, n):
        total = total + rsr[k]
    dpr[my_dp] = total

    def start_dp(k):
        pltpu.make_async_remote_copy(
            src_ref=dpr.at[my_dp],
            dst_ref=dpr.at[my_dp],
            send_sem=send_sems.at[5],
            recv_sem=recv_sems.at[5],
            device_id={"dp": wrap(my_dp + k, dps)},
            device_id_type=MESH,
        ).start()

    each_peer(dps, start_dp)

    for halo in halos:
        halo.wait()
    grad_columns(0)
    grad_columns(planes + 1)

    wait_bytes(dpr.at[pl.ds(0, dps - 1)], recv_sems.at[5])
    total = dpr[0]
    for k in range(1, dps):
        total = total + dpr[k]
    ag[me] = total * scale

    def start_ag(k):
        pltpu.make_async_remote_copy(
            src_ref=ag.at[me],
            dst_ref=ag.at[me],
            send_sem=send_sems.at[6],
            recv_sem=recv_sems.at[6],
            device_id={"gx": wrap(me + k, n)},
            device_id_type=MESH,
        ).start()

    each_peer(n, start_ag)

    grad_in = [
        mm(w_bwd, gcols[:, lane(x, y) : lane(x, y) + nz]).astype(bf16)
        for x in range(planes)
        for y in range(ny)
    ]
    gin_ref[...] = mm(back, jnp.concatenate(grad_in, axis=0)).astype(bf16)

    stores[1].start()
    wait_bytes(ag.at[pl.ds(0, n - 1)], recv_sems.at[6])
    for k in range(n):
        g, q = k % groups, k // groups
        gw_ref[g * per : g * per + per, q * 128 : q * 128 + 128] = ag[k]

    stores[2].start()
    wait_bytes(recv1.at[pl.ds(0, (n - 1) * planes)], send_sems.at[0])
    wait_bytes(recv2.at[pl.ds(0, chunks - 1), pl.ds(0, planes)], send_sems.at[1])
    wait_bytes(recv2.at[pl.ds(0, chunks - 1), pl.ds(planes, 2)], send_sems.at[7])
    wait_bytes(rsr.at[pl.ds(0, n - 1)], send_sems.at[4])
    wait_bytes(dpr.at[pl.ds(0, dps - 1)], send_sems.at[5])
    wait_bytes(ag.at[pl.ds(0, n - 1)], send_sems.at[6])
    for store in stores:
        store.wait()


def finish(
    ch, taps, hid_in, gin_in, gw_in, hid_out, gin_out, gw_out, gb_out,
    gw_ref, hid, gin, gw, gb, load_sems, sems,
):
    width = taps * ch
    loads = [
        pltpu.make_async_copy(source, target, load_sems.at[k])
        for k, (source, target) in enumerate([(hid_in, hid), (gin_in, gin), (gw_in, gw_ref)])
    ]
    for k in (2, 0, 1):
        loads[k].start()
    stores = [
        pltpu.make_async_copy(source, target, sems.at[k])
        for k, (source, target) in enumerate(
            [(hid, hid_out), (gin, gin_out), (gw, gw_out), (gb, gb_out)]
        )
    ]
    kept = iota((ch, 1), 0) == (iota((1, width), 1) & (ch - 1))
    tap_of = one_hot(iota((width, 1), 0) // ch == iota((1, taps), 1))
    for k in (2, 0, 1):
        loads[k].wait()
    stores[0].start()
    stores[1].start()
    pairs = jnp.concatenate(
        [jnp.where(kept, gw_ref[o : o + 1, 0:width], 0.0) for o in range(ch)], axis=0
    )
    high = pairs.astype(bf16)
    rest = pairs - high.astype(f32)
    mid = rest.astype(bf16)
    low = (rest - mid.astype(f32)).astype(bf16)
    gw[...] = mm(high, tap_of) + (mm(mid, tap_of) + mm(low, tap_of))
    stores[2].start()
    gb[...] = jnp.sum(
        jnp.where(iota((ch, 1), 0) == iota((1, ch), 1), gw_ref[:, width : width + 1], 0.0),
        axis=0, keepdims=True,
    )
    stores[3].start()
    for store in stores:
        store.wait()


def on_device(features, offsets, flip_bits, weight, conv_bias, cotangent):
    _, ch, planes, ny, nz = features.shape
    n, dps = lax.axis_size("gx"), lax.axis_size("dp")
    taps = weight.shape[0]
    rows, cells, chunks = ch * planes * ny, planes * ny * nz, ny * nz // 128
    width = taps * ch
    per = ch * 512 // (128 * n)
    scale = 1.0 / math.sqrt(dps * n * cells)
    vmem = pl.BlockSpec(memory_space=pltpu.VMEM)
    smem = pl.BlockSpec(memory_space=pltpu.SMEM)
    hbm = pl.BlockSpec(memory_space=pltpu.HBM)
    hidden, grad_in, grad_w = pl.pallas_call(
        functools.partial(kernel, n, dps, planes, ch, ny, nz, scale),
        out_shape=(
            jax.ShapeDtypeStruct((rows, nz), bf16),
            jax.ShapeDtypeStruct((rows, nz), bf16),
            jax.ShapeDtypeStruct((ch, 512), f32),
        ),
        in_specs=[smem, smem, hbm, hbm, vmem, hbm],
        out_specs=(hbm, hbm, hbm),
        scratch_shapes=[
            pltpu.VMEM((rows, nz), bf16),
            pltpu.VMEM((rows, nz), bf16),
            pltpu.VMEM((ch, 512), f32),
            pltpu.VMEM((rows, nz), bf16),
            pltpu.VMEM((ch * ch, taps), bf16),
            pltpu.VMEM((rows, nz), bf16),
            pltpu.VMEM((chunks, planes, ch, 128), bf16),
            pltpu.VMEM((n * planes, ch, 128), bf16),
            pltpu.VMEM((chunks, planes + 2, ch, 128), bf16),
            pltpu.VMEM((chunks, planes + 2, ch, 128), bf16),
            pltpu.VMEM((width + ch, cells), bf16),
            pltpu.VMEM((width, cells), bf16),
            pltpu.VMEM((planes + 2, ny, ch, nz), bf16),
            pltpu.VMEM((n, per, 128), f32),
            pltpu.VMEM((n, per, 128), f32),
            pltpu.VMEM((dps, per, 128), f32),
            pltpu.VMEM((n, per, 128), f32),
            pltpu.SemaphoreType.DMA((3,)),
            pltpu.SemaphoreType.DMA((3,)),
            pltpu.SemaphoreType.DMA((8,)),
            pltpu.SemaphoreType.DMA((8,)),
        ],
        compiler_params=pltpu.CompilerParams(
            collective_id=0, has_side_effects=True, vmem_limit_bytes=63 * 2**20
        ),
        cost_estimate=pl.CostEstimate(
            flops=6 * ch * width * cells, bytes_accessed=8 * rows * nz, transcendentals=2 * ch * cells
        ),
    )(
        offsets,
        flip_bits,
        features.reshape(rows, nz),
        weight.transpose(1, 2, 0).reshape(ch * ch, taps),
        conv_bias.reshape(1, ch),
        cotangent.reshape(rows, nz),
    )
    hidden, grad_in, grad_w, grad_b = pl.pallas_call(
        functools.partial(finish, ch, taps),
        out_shape=(
            jax.ShapeDtypeStruct((rows, nz), bf16),
            jax.ShapeDtypeStruct((rows, nz), bf16),
            jax.ShapeDtypeStruct((ch * ch, taps), f32),
            jax.ShapeDtypeStruct((1, ch), f32),
        ),
        in_specs=[hbm, hbm, hbm],
        out_specs=(hbm, hbm, hbm, hbm),
        scratch_shapes=[
            pltpu.VMEM((ch, 512), f32),
            pltpu.VMEM((rows, nz), bf16),
            pltpu.VMEM((rows, nz), bf16),
            pltpu.VMEM((ch * ch, taps), f32),
            pltpu.VMEM((1, ch), f32),
            pltpu.SemaphoreType.DMA((3,)),
            pltpu.SemaphoreType.DMA((4,)),
        ],
        compiler_params=pltpu.CompilerParams(vmem_limit_bytes=63 * 2**20),
    )(hidden, grad_in, grad_w)
    return (
        hidden.reshape(features.shape),
        grad_in.reshape(features.shape),
        grad_w.reshape(ch, ch, taps).transpose(2, 0, 1),
        grad_b.reshape(ch),
    )


def solution(mesh):
    in_specs = (
        P("dp", None, "gx", None, None),
        P("dp", None),
        P("dp", None),
        P(),
        P(),
        P("dp", None, "gx", None, None),
    )
    out_specs = (P("dp", None, "gx", None, None), P("dp", None, "gx", None, None), P(), P())
    return jax.shard_map(
        on_device, mesh=mesh, in_specs=in_specs, out_specs=out_specs, check_vma=False
    )
```

```python
import functools
import math

import jax
import jax.numpy as jnp
from jax import lax
from jax.experimental import pallas as pl
from jax.experimental.pallas import tpu as pltpu
from jax.sharding import PartitionSpec as P

MESH = pl.DeviceIdType.MESH
bf16, f32 = jnp.bfloat16, jnp.float32


def iota(shape, dim):
    return lax.broadcasted_iota(jnp.int32, shape, dim)


def one_hot(mask):
    return jnp.where(mask, 1.0, 0.0).astype(bf16)


def mm(a, b):
    return jnp.dot(a, b, preferred_element_type=f32)


def mm_t(a, b):
    return lax.dot_general(a, b, (((1,), (1,)), ((), ())), preferred_element_type=f32)


def gelu_parts(pre_act):
    normal_cdf = 0.5 * (1.0 + lax.erf(pre_act * 0.7071067811865476))
    density = jnp.exp(-0.5 * pre_act * pre_act) * 0.3989422804014327
    return (pre_act * normal_cdf, normal_cdf + pre_act * density)


def wrap(index, count):
    if count & (count - 1) == 0:
        return index & (count - 1)
    return lax.rem(index + count, count)


def each_peer(count, body):
    lax.fori_loop(1, count, lambda k, _: body(k) or 0, 0, unroll=count <= 16)


def wait_bytes(ref, sem):
    pltpu.make_async_copy(ref, ref, sem).wait()


def kernel(
    n, dps, planes, ch, ny, nz, scale,
    off_ref, flip_ref, feat_ref, weight_ref, bias_ref, cot_ref,
    hid_out, gin_out, gw_out,
    hid_ref, gin_ref, gw_ref, feat, weight, cot_in, send1, recv1, stag, recv2, cols, gcols, gext, rs, rsr, zr, ag,
    load_sems, store_sems, send_sems, recv_sems,
):
    me, my_dp = lax.axis_index("gx"), lax.axis_index("dp")
    taps = 27
    rows = ch * planes * ny
    chunks = ny * nz // 128
    nx = n * planes
    per = rs.shape[1]

    loads = [
        pltpu.make_async_copy(source, target, load_sems.at[k])
        for k, (source, target) in enumerate(
            [(feat_ref, feat), (weight_ref, weight), (cot_ref, cot_in)]
        )
    ]
    for load in loads:
        load.start()
    stores = [
        pltpu.make_async_copy(source, target, store_sems.at[k])
        for k, (source, target) in enumerate(
            [(hid_ref, hid_out), (gin_ref, gin_out), (gw_ref, gw_out)]
        )
    ]

    barrier = pltpu.get_barrier_semaphore()

    def greet(k):
        pl.semaphore_signal(
            barrier, inc=1, device_id={"gx": wrap(me + k, n)}, device_id_type=MESH
        )

    layer, heights = 4 * dps, n // 4
    low, high = me & 3, me // 4
    mine = my_dp * 4 + low

    def layer_peer(q):
        return {"dp": q // 4, "gx": high * 4 + (q & 3)}

    def greet_layer(k):
        pl.semaphore_signal(
            barrier, inc=1, device_id=layer_peer(wrap(my_dp * 4 + 3 + k, layer)), device_id_type=MESH
        )

    each_peer(n, greet)
    each_peer(layer - 3, greet_layer)

    r_out = iota((rows, 1), 0)
    r_in = iota((1, rows), 1)
    out_c, out_y, out_x = r_out & (ch - 1), (r_out // ch) & (ny - 1), r_out // (ch * ny)
    base = (out_c * planes + out_x) * ny
    src_y = jnp.where(flip_ref[0, 1] == 1, ny - 1 - out_y, out_y) - off_ref[0, 1]
    order = one_hot(r_in == base + out_y)
    order_aug = one_hot(r_in == base + (src_y & (ny - 1)))
    zi, zo = iota((nz, 1), 0), iota((1, nz), 1)
    src_z = jnp.where(flip_ref[0, 2] == 1, nz - 1 - zo, zo) - off_ref[0, 2]
    perm_z = one_hot(zi == (src_z & (nz - 1)))
    loads[0].wait()
    local = mm(feat[...], perm_z).astype(bf16)
    local = mm(order_aug, local).astype(bf16)
    for j in range(chunks):
        y, half = j // 2, j % 2
        for x in range(planes):
            r0 = (x * ny + y) * ch
            send1[j, x] = local[r0 : r0 + ch, half * 128 : half * 128 + 128]

    pl.semaphore_wait(barrier, n - 1 + layer - 4)

    def start1(k):
        peer = wrap(me + k, n)
        pltpu.make_async_remote_copy(
            src_ref=send1.at[wrap(peer, chunks)],
            dst_ref=recv1.at[pl.ds(me * planes, planes)],
            send_sem=send_sems.at[0],
            recv_sem=recv_sems.at[0],
            device_id={"gx": peer},
            device_id_type=MESH,
        ).start()

    each_peer(n, start1)
    my_chunk = wrap(me, chunks)
    group = me // chunks * chunks
    recv1[pl.ds(me * planes, planes)] = send1[my_chunk]

    width = taps * ch
    loads[1].wait()
    tap_of = one_hot(iota((taps, 1), 0) == iota((1, width), 1) // ch)
    spread = mm(weight[...], tap_of)
    pair, lane_c = iota((ch * ch, 1), 0), iota((1, width), 1) & (ch - 1)
    by_in = jnp.where((pair & (ch - 1)) == lane_c, spread, 0.0).astype(bf16)
    by_out = jnp.where(pair // ch == lane_c, spread, 0.0).astype(bf16)
    row, across = iota((ch, 1), 0), iota((1, ch * ch), 1)
    w_fwd = mm(one_hot(row == across // ch), by_in).astype(bf16)
    w_bwd = mm(one_hot(row == (across & (ch - 1))), by_out).astype(bf16)
    bias = jnp.sum(
        jnp.where(iota((ch, 1), 0) == iota((1, ch), 1), bias_ref[...], 0.0), axis=1, keepdims=True
    )
    z_less = one_hot(zi == ((zo - 1) & (nz - 1)))
    z_more = one_hot(zi == ((zo + 1) & (nz - 1)))
    cols[width : width + ch] = jnp.ones((ch, cols.shape[1]), bf16)
    loads[2].wait()
    cot = mm(order, cot_in[...])

    sources = []
    for p in range(chunks * planes + 2):
        target = wrap(group * planes + (p - 1), nx)
        source = jnp.where(flip_ref[0, 0] == 1, nx - 1 - target, target) - off_ref[0, 0]
        sources.append(wrap(source, nx))

    wait_bytes(recv1.at[pl.ds(0, (n - 1) * planes)], recv_sems.at[0])

    def routed(p):
        return recv1[sources[p]]

    first, last = planes, planes + 1
    for q in range(chunks):
        for x in range(planes):
            plane = routed(q * planes + x + 1)
            stag[q, x] = plane
            if x == planes - 1:
                stag[(q + 1) % chunks, first] = plane
            if x == 0:
                stag[(q - 1) % chunks, last] = plane
    stag[0, first] = routed(0)
    stag[chunks - 1, last] = routed(chunks * planes + 1)

    def start2(begin, count, k):
        q = wrap(my_chunk + k, chunks)
        pltpu.make_async_remote_copy(
            src_ref=stag.at[q, pl.ds(begin, count)],
            dst_ref=recv2.at[my_chunk, pl.ds(begin, count)],
            send_sem=send_sems.at[1 if begin == 0 else 7],
            recv_sem=recv_sems.at[1 if begin == 0 else 7],
            device_id={"gx": group + q},
            device_id_type=MESH,
        ).start()

    each_peer(chunks, functools.partial(start2, 0, planes))
    each_peer(chunks, functools.partial(start2, planes, 2))
    recv2[my_chunk] = stag[my_chunk]

    def lane(x, y):
        return (x * ny + y) * nz

    def columns(p):
        slot = first if p == 0 else last if p == planes + 1 else p - 1
        mid = [
            jnp.concatenate([recv2[2 * y, slot], recv2[2 * y + 1, slot]], axis=1)
            for y in range(ny)
        ]
        stacked = jnp.concatenate(mid, axis=0)
        shifts = [mm(stacked, z_less).astype(bf16), stacked, mm(stacked, z_more).astype(bf16)]
        for a in range(3):
            x = p - a
            if not 0 <= x < planes:
                continue
            for e in range(3):
                for h in range(3):
                    t = 9 * a + 3 * e + h
                    for y in range(ny):
                        s = (y + e - 1) % ny
                        cols[t * ch : t * ch + ch, lane(x, y) : lane(x, y) + nz] = shifts[h][
                            s * ch : s * ch + ch
                        ]

    wait_bytes(recv2.at[pl.ds(0, chunks - 1), pl.ds(0, planes)], recv_sems.at[1])
    for p in range(1, planes + 1):
        columns(p)

    part = []
    for x in range(planes):
        k0, k1 = max(0, 1 - x) * 9 * ch, min(3, planes + 1 - x) * 9 * ch
        for y in range(ny):
            at = slice(lane(x, y), lane(x, y) + nz)
            part.append(mm(w_fwd[:, k0:k1], cols[k0:k1, at]) + bias)

    wait_bytes(recv2.at[pl.ds(0, chunks - 1), pl.ds(planes, 2)], recv_sems.at[7])
    columns(0)
    columns(planes + 1)

    hidden = []
    for x in range(planes):
        for y in range(ny):
            r0 = (x * ny + y) * ch
            at = slice(lane(x, y), lane(x, y) + nz)
            pre = part[x * ny + y]
            if x == 0:
                pre = pre + mm(w_fwd[:, : 9 * ch], cols[: 9 * ch, at])
            if x == planes - 1:
                pre = pre + mm(w_fwd[:, 18 * ch :], cols[18 * ch : width, at])
            act, slope = gelu_parts(pre)
            hidden.append(act.astype(bf16))
            gext[x + 1, y] = (cot[r0 : r0 + ch] * slope).astype(bf16)

    right, left = lax.rem(me + 1, n), lax.rem(me + n - 1, n)
    halos = [
        pltpu.make_async_remote_copy(
            src_ref=gext.at[here],
            dst_ref=gext.at[there],
            send_sem=send_sems.at[2 + side],
            recv_sem=recv_sems.at[2 + side],
            device_id={"gx": peer},
            device_id_type=MESH,
        )
        for side, (here, there, peer) in enumerate(
            [(planes, 0, right), (1, planes + 1, left)]
        )
    ]
    gw = jnp.zeros((ch, width + ch), f32)
    for x in range(planes):
        for y in range(ny):
            gw = gw + mm_t(gext[x + 1, y], cols[:, lane(x, y) : lane(x, y) + nz])
    gw = jnp.concatenate([gw, jnp.zeros((ch, 512 - width - ch), f32)], axis=1)
    groups = ch // per
    for k in range(layer):
        g, q = k % groups, k // groups
        rs[k] = gw[g * per : g * per + per, q * 128 : q * 128 + 128]

    def start_rs(k):
        peer = wrap(mine + k, layer)
        pltpu.make_async_remote_copy(
            src_ref=rs.at[peer],
            dst_ref=rsr.at[mine],
            send_sem=send_sems.at[4],
            recv_sem=recv_sems.at[4],
            device_id=layer_peer(peer),
            device_id_type=MESH,
        ).start()

    each_peer(layer, start_rs)
    rsr[mine] = rs[mine]
    for halo in halos:
        halo.start()

    b_out, b_in = iota((rows, 1), 0), iota((1, rows), 1)
    b_base = ((b_in & (ch - 1)) * planes + b_in // (ch * ny)) * ny
    back = one_hot(b_out == b_base + ((b_in // ch) & (ny - 1)))
    hid_ref[...] = mm(back, jnp.concatenate(hidden, axis=0)).astype(bf16)
    stores[0].start()

    def grad_columns(p):
        stacked = jnp.concatenate([gext[p, y] for y in range(ny)], axis=0)
        shifts = [mm(stacked, z_more).astype(bf16), stacked, mm(stacked, z_less).astype(bf16)]
        for a in range(3):
            x = p + a - 2
            if not 0 <= x < planes:
                continue
            for e in range(3):
                for h in range(3):
                    t = 9 * a + 3 * e + h
                    for y in range(ny):
                        s = (y + 1 - e) % ny
                        gcols[t * ch : t * ch + ch, lane(x, y) : lane(x, y) + nz] = shifts[h][
                            s * ch : s * ch + ch
                        ]

    for p in range(1, planes + 1):
        grad_columns(p)

    wait_bytes(rsr.at[pl.ds(0, layer - 1)], recv_sems.at[4])
    total = rsr[0]
    for k in range(1, layer):
        total = total + rsr[k]
    zr[high] = total

    def start_z(k):
        pltpu.make_async_remote_copy(
            src_ref=zr.at[high],
            dst_ref=zr.at[high],
            send_sem=send_sems.at[5],
            recv_sem=recv_sems.at[5],
            device_id={"gx": wrap(high + k, heights) * 4 + low},
            device_id_type=MESH,
        ).start()

    each_peer(heights, start_z)

    for halo in halos:
        halo.wait()
    grad_columns(0)
    grad_columns(planes + 1)

    wait_bytes(zr.at[pl.ds(0, heights - 1)], recv_sems.at[5])
    total = zr[0]
    for k in range(1, heights):
        total = total + zr[k]
    ag[mine] = total * scale

    def start_ag(k):
        pltpu.make_async_remote_copy(
            src_ref=ag.at[mine],
            dst_ref=ag.at[mine],
            send_sem=send_sems.at[6],
            recv_sem=recv_sems.at[6],
            device_id=layer_peer(wrap(mine + k, layer)),
            device_id_type=MESH,
        ).start()

    each_peer(layer, start_ag)

    grad_in = [
        mm(w_bwd, gcols[:, lane(x, y) : lane(x, y) + nz]).astype(bf16)
        for x in range(planes)
        for y in range(ny)
    ]
    gin_ref[...] = mm(back, jnp.concatenate(grad_in, axis=0)).astype(bf16)

    stores[1].start()
    wait_bytes(ag.at[pl.ds(0, layer - 1)], recv_sems.at[6])
    for k in range(layer):
        g, q = k % groups, k // groups
        gw_ref[g * per : g * per + per, q * 128 : q * 128 + 128] = ag[k]

    stores[2].start()
    wait_bytes(recv1.at[pl.ds(0, (n - 1) * planes)], send_sems.at[0])
    wait_bytes(recv2.at[pl.ds(0, chunks - 1), pl.ds(0, planes)], send_sems.at[1])
    wait_bytes(recv2.at[pl.ds(0, chunks - 1), pl.ds(planes, 2)], send_sems.at[7])
    wait_bytes(rsr.at[pl.ds(0, layer - 1)], send_sems.at[4])
    wait_bytes(zr.at[pl.ds(0, heights - 1)], send_sems.at[5])
    wait_bytes(ag.at[pl.ds(0, layer - 1)], send_sems.at[6])
    for store in stores:
        store.wait()


def finish(
    ch, taps, hid_in, gin_in, gw_in, hid_out, gin_out, gw_out, gb_out,
    gw_ref, hid, gin, gw, gb, load_sems, sems,
):
    width = taps * ch
    loads = [
        pltpu.make_async_copy(source, target, load_sems.at[k])
        for k, (source, target) in enumerate([(hid_in, hid), (gin_in, gin), (gw_in, gw_ref)])
    ]
    for k in (2, 0, 1):
        loads[k].start()
    stores = [
        pltpu.make_async_copy(source, target, sems.at[k])
        for k, (source, target) in enumerate(
            [(hid, hid_out), (gin, gin_out), (gw, gw_out), (gb, gb_out)]
        )
    ]
    kept = iota((ch, 1), 0) == (iota((1, width), 1) & (ch - 1))
    tap_of = one_hot(iota((width, 1), 0) // ch == iota((1, taps), 1))
    for k in (2, 0, 1):
        loads[k].wait()
    stores[0].start()
    stores[1].start()
    pairs = jnp.concatenate(
        [jnp.where(kept, gw_ref[o : o + 1, 0:width], 0.0) for o in range(ch)], axis=0
    )
    high = pairs.astype(bf16)
    rest = pairs - high.astype(f32)
    mid = rest.astype(bf16)
    low = (rest - mid.astype(f32)).astype(bf16)
    gw[...] = mm(high, tap_of) + (mm(mid, tap_of) + mm(low, tap_of))
    stores[2].start()
    gb[...] = jnp.sum(
        jnp.where(iota((ch, 1), 0) == iota((1, ch), 1), gw_ref[:, width : width + 1], 0.0),
        axis=0, keepdims=True,
    )
    stores[3].start()
    for store in stores:
        store.wait()


def on_device(features, offsets, flip_bits, weight, conv_bias, cotangent):
    _, ch, planes, ny, nz = features.shape
    n, dps = lax.axis_size("gx"), lax.axis_size("dp")
    taps = weight.shape[0]
    rows, cells, chunks = ch * planes * ny, planes * ny * nz, ny * nz // 128
    width = taps * ch
    layer = 4 * dps
    per = ch * 512 // (128 * layer)
    scale = 1.0 / math.sqrt(dps * n * cells)
    vmem = pl.BlockSpec(memory_space=pltpu.VMEM)
    smem = pl.BlockSpec(memory_space=pltpu.SMEM)
    hbm = pl.BlockSpec(memory_space=pltpu.HBM)
    hidden, grad_in, grad_w = pl.pallas_call(
        functools.partial(kernel, n, dps, planes, ch, ny, nz, scale),
        out_shape=(
            jax.ShapeDtypeStruct((rows, nz), bf16),
            jax.ShapeDtypeStruct((rows, nz), bf16),
            jax.ShapeDtypeStruct((ch, 512), f32),
        ),
        in_specs=[smem, smem, hbm, hbm, vmem, hbm],
        out_specs=(hbm, hbm, hbm),
        scratch_shapes=[
            pltpu.VMEM((rows, nz), bf16),
            pltpu.VMEM((rows, nz), bf16),
            pltpu.VMEM((ch, 512), f32),
            pltpu.VMEM((rows, nz), bf16),
            pltpu.VMEM((ch * ch, taps), bf16),
            pltpu.VMEM((rows, nz), bf16),
            pltpu.VMEM((chunks, planes, ch, 128), bf16),
            pltpu.VMEM((n * planes, ch, 128), bf16),
            pltpu.VMEM((chunks, planes + 2, ch, 128), bf16),
            pltpu.VMEM((chunks, planes + 2, ch, 128), bf16),
            pltpu.VMEM((width + ch, cells), bf16),
            pltpu.VMEM((width, cells), bf16),
            pltpu.VMEM((planes + 2, ny, ch, nz), bf16),
            pltpu.VMEM((layer, per, 128), f32),
            pltpu.VMEM((layer, per, 128), f32),
            pltpu.VMEM((n // 4, per, 128), f32),
            pltpu.VMEM((layer, per, 128), f32),
            pltpu.SemaphoreType.DMA((3,)),
            pltpu.SemaphoreType.DMA((3,)),
            pltpu.SemaphoreType.DMA((8,)),
            pltpu.SemaphoreType.DMA((8,)),
        ],
        compiler_params=pltpu.CompilerParams(
            collective_id=0, has_side_effects=True, vmem_limit_bytes=63 * 2**20
        ),
        cost_estimate=pl.CostEstimate(
            flops=6 * ch * width * cells, bytes_accessed=8 * rows * nz, transcendentals=2 * ch * cells
        ),
    )(
        offsets,
        flip_bits,
        features.reshape(rows, nz),
        weight.transpose(1, 2, 0).reshape(ch * ch, taps),
        conv_bias.reshape(1, ch),
        cotangent.reshape(rows, nz),
    )
    hidden, grad_in, grad_w, grad_b = pl.pallas_call(
        functools.partial(finish, ch, taps),
        out_shape=(
            jax.ShapeDtypeStruct((rows, nz), bf16),
            jax.ShapeDtypeStruct((rows, nz), bf16),
            jax.ShapeDtypeStruct((ch * ch, taps), f32),
            jax.ShapeDtypeStruct((1, ch), f32),
        ),
        in_specs=[hbm, hbm, hbm],
        out_specs=(hbm, hbm, hbm, hbm),
        scratch_shapes=[
            pltpu.VMEM((ch, 512), f32),
            pltpu.VMEM((rows, nz), bf16),
            pltpu.VMEM((rows, nz), bf16),
            pltpu.VMEM((ch * ch, taps), f32),
            pltpu.VMEM((1, ch), f32),
            pltpu.SemaphoreType.DMA((3,)),
            pltpu.SemaphoreType.DMA((4,)),
        ],
        compiler_params=pltpu.CompilerParams(vmem_limit_bytes=63 * 2**20),
    )(hidden, grad_in, grad_w)
    return (
        hidden.reshape(features.shape),
        grad_in.reshape(features.shape),
        grad_w.reshape(ch, ch, taps).transpose(2, 0, 1),
        grad_b.reshape(ch),
    )


def solution(mesh):
    in_specs = (
        P("dp", None, "gx", None, None),
        P("dp", None),
        P("dp", None),
        P(),
        P(),
        P("dp", None, "gx", None, None),
    )
    out_specs = (P("dp", None, "gx", None, None), P("dp", None, "gx", None, None), P(), P())
    return jax.shard_map(
        on_device, mesh=mesh, in_specs=in_specs, out_specs=out_specs, check_vma=False
    )
```

```python
import functools
import math

import jax
import jax.numpy as jnp
from jax import lax
from jax.experimental import pallas as pl
from jax.experimental.pallas import tpu as pltpu
from jax.sharding import PartitionSpec as P

MESH = pl.DeviceIdType.MESH
bf16, f32 = jnp.bfloat16, jnp.float32


def iota(shape, dim):
    return lax.broadcasted_iota(jnp.int32, shape, dim)


def one_hot(mask):
    return jnp.where(mask, 1.0, 0.0).astype(bf16)


def mm(a, b):
    return jnp.dot(a, b, preferred_element_type=f32)


def mm_t(a, b):
    return lax.dot_general(a, b, (((1,), (1,)), ((), ())), preferred_element_type=f32)


def gelu_parts(pre_act):
    normal_cdf = 0.5 * (1.0 + lax.erf(pre_act * 0.7071067811865476))
    density = jnp.exp(-0.5 * pre_act * pre_act) * 0.3989422804014327
    return (pre_act * normal_cdf, normal_cdf + pre_act * density)


def wrap(index, count):
    if count & (count - 1) == 0:
        return index & (count - 1)
    return lax.rem(index + count, count)


def each_peer(count, body):
    lax.fori_loop(1, count, lambda k, _: body(k) or 0, 0, unroll=count <= 16)


def wait_bytes(ref, sem):
    pltpu.make_async_copy(ref, ref, sem).wait()


def kernel(
    n, dps, planes, ch, ny, nz, scale,
    off_ref, flip_ref, feat_ref, weight_ref, bias_ref, cot_ref,
    hid_out, gin_out, gw_out,
    hid_ref, gin_ref, gw_ref, feat, weight, cot_in, send1, recv1, stag, recv2,
    zs, gz, wf, wb, shift, cot, hid, gin, gext, rs, rsr, zr, ag,
    load_sems, store_sems, send_sems, recv_sems,
):
    me, my_dp = lax.axis_index("gx"), lax.axis_index("dp")
    taps = 27
    rows = ch * planes * ny
    chunks = ny * nz // 128
    nx = n * planes
    per = rs.shape[1]

    loads = [
        pltpu.make_async_copy(source, target, load_sems.at[k])
        for k, (source, target) in enumerate(
            [(feat_ref, feat), (weight_ref, weight), (cot_ref, cot_in)]
        )
    ]
    for load in loads:
        load.start()
    stores = [
        pltpu.make_async_copy(source, target, store_sems.at[k])
        for k, (source, target) in enumerate(
            [(hid_ref, hid_out), (gin_ref, gin_out), (gw_ref, gw_out)]
        )
    ]

    barrier = pltpu.get_barrier_semaphore()

    def greet(k):
        pl.semaphore_signal(
            barrier, inc=1, device_id={"gx": wrap(me + k, n)}, device_id_type=MESH
        )

    layer, heights = 4 * dps, n // 4
    low, high = me & 3, me // 4
    mine = my_dp * 4 + low

    def layer_peer(q):
        return {"dp": q // 4, "gx": high * 4 + (q & 3)}

    def greet_layer(k):
        pl.semaphore_signal(
            barrier, inc=1, device_id=layer_peer(wrap(my_dp * 4 + 3 + k, layer)), device_id_type=MESH
        )

    each_peer(n, greet)
    each_peer(layer - 3, greet_layer)

    r_out = iota((rows, 1), 0)
    r_in = iota((1, rows), 1)
    out_c, out_y, out_x = r_out & (ch - 1), (r_out // ch) & (ny - 1), r_out // (ch * ny)
    base = (out_c * planes + out_x) * ny
    src_y = jnp.where(flip_ref[0, 1] == 1, ny - 1 - out_y, out_y) - off_ref[0, 1]
    order = one_hot(r_in == base + out_y)
    order_aug = one_hot(r_in == base + (src_y & (ny - 1)))
    zi, zo = iota((nz, 1), 0), iota((1, nz), 1)
    src_z = jnp.where(flip_ref[0, 2] == 1, nz - 1 - zo, zo) - off_ref[0, 2]
    perm_z = one_hot(zi == (src_z & (nz - 1)))
    loads[0].wait()
    local = mm(feat[...], perm_z).astype(bf16)
    local = mm(order_aug, local).astype(bf16)
    for j in range(chunks):
        y, half = j // 2, j % 2
        for x in range(planes):
            r0 = (x * ny + y) * ch
            send1[j, x] = local[r0 : r0 + ch, half * 128 : half * 128 + 128]

    pl.semaphore_wait(barrier, n - 1 + layer - 4)

    def start1(k):
        peer = wrap(me + k, n)
        pltpu.make_async_remote_copy(
            src_ref=send1.at[wrap(peer, chunks)],
            dst_ref=recv1.at[pl.ds(me * planes, planes)],
            send_sem=send_sems.at[0],
            recv_sem=recv_sems.at[0],
            device_id={"gx": peer},
            device_id_type=MESH,
        ).start()

    each_peer(n, start1)
    my_chunk = wrap(me, chunks)
    group = me // chunks * chunks
    recv1[pl.ds(me * planes, planes)] = send1[my_chunk]

    width = taps * ch
    loads[1].wait()
    tap_of = one_hot(iota((taps, 1), 0) == iota((1, width), 1) // ch)
    spread = mm(weight[...], tap_of)
    pair, lane_c = iota((ch * ch, 1), 0), iota((1, width), 1) & (ch - 1)
    by_in = jnp.where((pair & (ch - 1)) == lane_c, spread, 0.0).astype(bf16)
    by_out = jnp.where(pair // ch == lane_c, spread, 0.0).astype(bf16)
    row, across = iota((ch, 1), 0), iota((1, ch * ch), 1)
    w_fwd = mm(one_hot(row == across // ch), by_in).astype(bf16)
    w_bwd = mm(one_hot(row == (across & (ch - 1))), by_out).astype(bf16)
    bias = jnp.sum(
        jnp.where(iota((ch, 1), 0) == iota((1, ch), 1), bias_ref[...], 0.0), axis=1, keepdims=True
    )
    for k in range(9):
        wf[k] = w_fwd[:, k * 3 * ch : (k + 1) * 3 * ch]
        wb[k] = w_bwd[:, k * 3 * ch : (k + 1) * 3 * ch]
    shift[0] = one_hot(zi == ((zo - 1) & (nz - 1)))
    shift[1] = one_hot(zi == ((zo + 1) & (nz - 1)))
    loads[2].wait()
    cot[...] = mm(order, cot_in[...]).reshape(cot.shape)

    sources = []
    for p in range(chunks * planes + 2):
        target = wrap(group * planes + (p - 1), nx)
        source = jnp.where(flip_ref[0, 0] == 1, nx - 1 - target, target) - off_ref[0, 0]
        sources.append(wrap(source, nx))

    wait_bytes(recv1.at[pl.ds(0, (n - 1) * planes)], recv_sems.at[0])

    def routed(p):
        return recv1[sources[p]]

    first, last = planes + 1, planes
    for q in range(chunks):
        for x in range(planes):
            plane = routed(q * planes + x + 1)
            stag[q, x] = plane
            if x == planes - 1:
                stag[(q + 1) % chunks, first] = plane
            if x == 0:
                stag[(q - 1) % chunks, last] = plane
    stag[0, first] = routed(0)
    stag[chunks - 1, last] = routed(chunks * planes + 1)

    def start2(begin, count, k):
        q = wrap(my_chunk + k, chunks)
        pltpu.make_async_remote_copy(
            src_ref=stag.at[q, pl.ds(begin, count)],
            dst_ref=recv2.at[my_chunk, pl.ds(begin, count)],
            send_sem=send_sems.at[1 if begin == 0 else 7],
            recv_sem=recv_sems.at[1 if begin == 0 else 7],
            device_id={"gx": group + q},
            device_id_type=MESH,
        ).start()

    each_peer(chunks, functools.partial(start2, 0, planes))
    each_peer(chunks, functools.partial(start2, planes, 2))
    recv2[my_chunk] = stag[my_chunk]

    def build(target, block, slot, less):
        stacked = jnp.concatenate([block(slot, y) for y in range(ny)], axis=0)
        shifted = [
            mm(stacked, shift[less]).astype(bf16),
            stacked,
            mm(stacked, shift[1 - less]).astype(bf16),
        ]
        for y in range(ny):
            for h in range(3):
                target[slot, y, h * ch : h * ch + ch] = shifted[h][y * ch : y * ch + ch]

    def build_forward(slot, _):
        build(
            zs,
            lambda at, y: jnp.concatenate([recv2[2 * y, at], recv2[2 * y + 1, at]], axis=1),
            slot, 0,
        )
        return 0

    def build_backward(slot, _):
        build(gz, lambda at, y: gext[at, y], slot, 1)
        return 0

    step = 4
    per_plane = ny // step
    pairs = [(a, e) for a in range(3) for e in range(3)]

    def conv_blocks(i, sums):
        sums = list(sums)
        x, y0 = i // per_plane, (i % per_plane) * step
        for j in range(step):
            y = y0 + j
            at = [(lax.rem(x + a + planes + 1, planes + 2), (y + e - 1) & (ny - 1)) for a, e in pairs]
            pre = bias
            for k in range(9):
                pre = pre + mm(wf[k], zs[at[k]])
            act, slope = gelu_parts(pre)
            hid[x * ny + y] = act.astype(bf16)
            grad = (cot[x * ny + y] * slope).astype(bf16)
            gext[x, y] = grad
            for k in range(9):
                sums[k] = sums[k] + mm_t(grad, zs[at[k]])
            sums[9] = sums[9] + grad.astype(f32)
        return tuple(sums)

    def grad_blocks(i, _):
        x, y0 = i // per_plane, (i % per_plane) * step
        for j in range(step):
            y = y0 + j
            total = jnp.zeros((ch, nz), f32)
            for k, (a, e) in enumerate(pairs):
                slot = lax.rem(x + planes + 3 - a, planes + 2)
                total = total + mm(wb[k], gz[slot, (y + 1 - e) & (ny - 1)])
            gin[x * ny + y] = total.astype(bf16)
        return 0

    wait_bytes(recv2.at[pl.ds(0, chunks - 1), pl.ds(0, planes)], recv_sems.at[1])
    lax.fori_loop(0, planes, build_forward, 0)
    wait_bytes(recv2.at[pl.ds(0, chunks - 1), pl.ds(planes, 2)], recv_sems.at[7])
    lax.fori_loop(planes, planes + 2, build_forward, 0)
    zeros = (jnp.zeros((ch, 3 * ch), f32),) * 9 + (jnp.zeros((ch, nz), f32),)
    sums = lax.fori_loop(0, planes * per_plane, conv_blocks, zeros)

    right, left = lax.rem(me + 1, n), lax.rem(me + n - 1, n)
    halos = [
        pltpu.make_async_remote_copy(
            src_ref=gext.at[here],
            dst_ref=gext.at[there],
            send_sem=send_sems.at[2 + side],
            recv_sem=recv_sems.at[2 + side],
            device_id={"gx": peer},
            device_id_type=MESH,
        )
        for side, (here, there, peer) in enumerate(
            [(planes - 1, planes + 1, right), (0, planes, left)]
        )
    ]
    gw = jnp.concatenate(
        list(sums[:9])
        + [jnp.sum(sums[9], axis=1, keepdims=True), jnp.zeros((ch, 511 - width), f32)],
        axis=1,
    )
    groups = ch // per
    for k in range(layer):
        g, q = k % groups, k // groups
        rs[k] = gw[g * per : g * per + per, q * 128 : q * 128 + 128]

    def start_rs(k):
        peer = wrap(mine + k, layer)
        pltpu.make_async_remote_copy(
            src_ref=rs.at[peer],
            dst_ref=rsr.at[mine],
            send_sem=send_sems.at[4],
            recv_sem=recv_sems.at[4],
            device_id=layer_peer(peer),
            device_id_type=MESH,
        ).start()

    each_peer(layer, start_rs)
    rsr[mine] = rs[mine]
    for halo in halos:
        halo.start()

    b_out, b_in = iota((rows, 1), 0), iota((1, rows), 1)
    b_base = ((b_in & (ch - 1)) * planes + b_in // (ch * ny)) * ny
    back = one_hot(b_out == b_base + ((b_in // ch) & (ny - 1)))
    hid_ref[...] = mm(back, hid[...].reshape(rows, nz)).astype(bf16)
    stores[0].start()

    lax.fori_loop(0, planes, build_backward, 0)

    wait_bytes(rsr.at[pl.ds(0, layer - 1)], recv_sems.at[4])
    total = rsr[0]
    for k in range(1, layer):
        total = total + rsr[k]
    zr[high] = total

    def start_z(k):
        pltpu.make_async_remote_copy(
            src_ref=zr.at[high],
            dst_ref=zr.at[high],
            send_sem=send_sems.at[5],
            recv_sem=recv_sems.at[5],
            device_id={"gx": wrap(high + k, heights) * 4 + low},
            device_id_type=MESH,
        ).start()

    each_peer(heights, start_z)

    for halo in halos:
        halo.wait()
    lax.fori_loop(planes, planes + 2, build_backward, 0)

    wait_bytes(zr.at[pl.ds(0, heights - 1)], recv_sems.at[5])
    total = zr[0]
    for k in range(1, heights):
        total = total + zr[k]
    ag[mine] = total * scale

    def start_ag(k):
        pltpu.make_async_remote_copy(
            src_ref=ag.at[mine],
            dst_ref=ag.at[mine],
            send_sem=send_sems.at[6],
            recv_sem=recv_sems.at[6],
            device_id=layer_peer(wrap(mine + k, layer)),
            device_id_type=MESH,
        ).start()

    each_peer(layer, start_ag)

    lax.fori_loop(0, planes * per_plane, grad_blocks, 0)
    gin_ref[...] = mm(back, gin[...].reshape(rows, nz)).astype(bf16)

    stores[1].start()
    wait_bytes(ag.at[pl.ds(0, layer - 1)], recv_sems.at[6])
    for k in range(layer):
        g, q = k % groups, k // groups
        gw_ref[g * per : g * per + per, q * 128 : q * 128 + 128] = ag[k]

    stores[2].start()
    wait_bytes(recv1.at[pl.ds(0, (n - 1) * planes)], send_sems.at[0])
    wait_bytes(recv2.at[pl.ds(0, chunks - 1), pl.ds(0, planes)], send_sems.at[1])
    wait_bytes(recv2.at[pl.ds(0, chunks - 1), pl.ds(planes, 2)], send_sems.at[7])
    wait_bytes(rsr.at[pl.ds(0, layer - 1)], send_sems.at[4])
    wait_bytes(zr.at[pl.ds(0, heights - 1)], send_sems.at[5])
    wait_bytes(ag.at[pl.ds(0, layer - 1)], send_sems.at[6])
    for store in stores:
        store.wait()


def finish(
    ch, taps, hid_in, gin_in, gw_in, hid_out, gin_out, gw_out, gb_out,
    gw_ref, hid, gin, gw, gb, load_sems, sems,
):
    width = taps * ch
    loads = [
        pltpu.make_async_copy(source, target, load_sems.at[k])
        for k, (source, target) in enumerate([(hid_in, hid), (gin_in, gin), (gw_in, gw_ref)])
    ]
    for k in (2, 0, 1):
        loads[k].start()
    stores = [
        pltpu.make_async_copy(source, target, sems.at[k])
        for k, (source, target) in enumerate(
            [(hid, hid_out), (gin, gin_out), (gw, gw_out), (gb, gb_out)]
        )
    ]
    kept = iota((ch, 1), 0) == (iota((1, width), 1) & (ch - 1))
    tap_of = one_hot(iota((width, 1), 0) // ch == iota((1, taps), 1))
    for k in (2, 0, 1):
        loads[k].wait()
    stores[0].start()
    stores[1].start()
    pairs = jnp.concatenate(
        [jnp.where(kept, gw_ref[o : o + 1, 0:width], 0.0) for o in range(ch)], axis=0
    )
    high = pairs.astype(bf16)
    rest = pairs - high.astype(f32)
    mid = rest.astype(bf16)
    low = (rest - mid.astype(f32)).astype(bf16)
    gw[...] = mm(high, tap_of) + (mm(mid, tap_of) + mm(low, tap_of))
    stores[2].start()
    gb[...] = jnp.sum(
        jnp.where(iota((ch, 1), 0) == iota((1, ch), 1), gw_ref[:, width : width + 1], 0.0),
        axis=0, keepdims=True,
    )
    stores[3].start()
    for store in stores:
        store.wait()


def on_device(features, offsets, flip_bits, weight, conv_bias, cotangent):
    _, ch, planes, ny, nz = features.shape
    n, dps = lax.axis_size("gx"), lax.axis_size("dp")
    taps = weight.shape[0]
    rows, cells, chunks = ch * planes * ny, planes * ny * nz, ny * nz // 128
    width = taps * ch
    layer = 4 * dps
    per = ch * 512 // (128 * layer)
    scale = 1.0 / math.sqrt(dps * n * cells)
    vmem = pl.BlockSpec(memory_space=pltpu.VMEM)
    smem = pl.BlockSpec(memory_space=pltpu.SMEM)
    hbm = pl.BlockSpec(memory_space=pltpu.HBM)
    hidden, grad_in, grad_w = pl.pallas_call(
        functools.partial(kernel, n, dps, planes, ch, ny, nz, scale),
        out_shape=(
            jax.ShapeDtypeStruct((rows, nz), bf16),
            jax.ShapeDtypeStruct((rows, nz), bf16),
            jax.ShapeDtypeStruct((ch, 512), f32),
        ),
        in_specs=[smem, smem, hbm, hbm, vmem, hbm],
        out_specs=(hbm, hbm, hbm),
        scratch_shapes=[
            pltpu.VMEM((rows, nz), bf16),
            pltpu.VMEM((rows, nz), bf16),
            pltpu.VMEM((ch, 512), f32),
            pltpu.VMEM((rows, nz), bf16),
            pltpu.VMEM((ch * ch, taps), bf16),
            pltpu.VMEM((rows, nz), bf16),
            pltpu.VMEM((chunks, planes, ch, 128), bf16),
            pltpu.VMEM((n * planes, ch, 128), bf16),
            pltpu.VMEM((chunks, planes + 2, ch, 128), bf16),
            pltpu.VMEM((chunks, planes + 2, ch, 128), bf16),
            pltpu.VMEM((planes + 2, ny, 3 * ch, nz), bf16),
            pltpu.VMEM((planes + 2, ny, 3 * ch, nz), bf16),
            pltpu.VMEM((9, ch, 3 * ch), bf16),
            pltpu.VMEM((9, ch, 3 * ch), bf16),
            pltpu.VMEM((2, nz, nz), bf16),
            pltpu.VMEM((planes * ny, ch, nz), f32),
            pltpu.VMEM((planes * ny, ch, nz), bf16),
            pltpu.VMEM((planes * ny, ch, nz), bf16),
            pltpu.VMEM((planes + 2, ny, ch, nz), bf16),
            pltpu.VMEM((layer, per, 128), f32),
            pltpu.VMEM((layer, per, 128), f32),
            pltpu.VMEM((n // 4, per, 128), f32),
            pltpu.VMEM((layer, per, 128), f32),
            pltpu.SemaphoreType.DMA((3,)),
            pltpu.SemaphoreType.DMA((3,)),
            pltpu.SemaphoreType.DMA((8,)),
            pltpu.SemaphoreType.DMA((8,)),
        ],
        compiler_params=pltpu.CompilerParams(
            collective_id=0, has_side_effects=True, vmem_limit_bytes=63 * 2**20
        ),
        cost_estimate=pl.CostEstimate(
            flops=6 * ch * width * cells, bytes_accessed=8 * rows * nz, transcendentals=2 * ch * cells
        ),
    )(
        offsets,
        flip_bits,
        features.reshape(rows, nz),
        weight.transpose(1, 2, 0).reshape(ch * ch, taps),
        conv_bias.reshape(1, ch),
        cotangent.reshape(rows, nz),
    )
    hidden, grad_in, grad_w, grad_b = pl.pallas_call(
        functools.partial(finish, ch, taps),
        out_shape=(
            jax.ShapeDtypeStruct((rows, nz), bf16),
            jax.ShapeDtypeStruct((rows, nz), bf16),
            jax.ShapeDtypeStruct((ch * ch, taps), f32),
            jax.ShapeDtypeStruct((1, ch), f32),
        ),
        in_specs=[hbm, hbm, hbm],
        out_specs=(hbm, hbm, hbm, hbm),
        scratch_shapes=[
            pltpu.VMEM((ch, 512), f32),
            pltpu.VMEM((rows, nz), bf16),
            pltpu.VMEM((rows, nz), bf16),
            pltpu.VMEM((ch * ch, taps), f32),
            pltpu.VMEM((1, ch), f32),
            pltpu.SemaphoreType.DMA((3,)),
            pltpu.SemaphoreType.DMA((4,)),
        ],
        compiler_params=pltpu.CompilerParams(vmem_limit_bytes=63 * 2**20),
    )(hidden, grad_in, grad_w)
    return (
        hidden.reshape(features.shape),
        grad_in.reshape(features.shape),
        grad_w.reshape(ch, ch, taps).transpose(2, 0, 1),
        grad_b.reshape(ch),
    )


def solution(mesh):
    in_specs = (
        P("dp", None, "gx", None, None),
        P("dp", None),
        P("dp", None),
        P(),
        P(),
        P("dp", None, "gx", None, None),
    )
    out_specs = (P("dp", None, "gx", None, None), P("dp", None, "gx", None, None), P(), P())
    return jax.shard_map(
        on_device, mesh=mesh, in_specs=in_specs, out_specs=out_specs, check_vma=False
    )
```

```python
import functools
import math

import jax
import jax.numpy as jnp
from jax import lax
from jax.experimental import pallas as pl
from jax.experimental.pallas import tpu as pltpu
from jax.sharding import PartitionSpec as P

MESH = pl.DeviceIdType.MESH
bf16, f32 = jnp.bfloat16, jnp.float32


def iota(shape, dim):
    return lax.broadcasted_iota(jnp.int32, shape, dim)


def one_hot(mask):
    return jnp.where(mask, 1.0, 0.0).astype(bf16)


def mm(a, b):
    return jnp.dot(a, b, preferred_element_type=f32)


def mm_t(a, b):
    return lax.dot_general(a, b, (((1,), (1,)), ((), ())), preferred_element_type=f32)


def gelu_parts(pre_act):
    normal_cdf = 0.5 * (1.0 + lax.erf(pre_act * 0.7071067811865476))
    density = jnp.exp(-0.5 * pre_act * pre_act) * 0.3989422804014327
    return (pre_act * normal_cdf, normal_cdf + pre_act * density)


def wrap(index, count):
    if count & (count - 1) == 0:
        return index & (count - 1)
    return lax.rem(index + count, count)


def each_peer(count, body):
    lax.fori_loop(1, count, lambda k, _: body(k) or 0, 0, unroll=count <= 16)


def wait_bytes(ref, sem):
    pltpu.make_async_copy(ref, ref, sem).wait()


def kernel(
    n, dps, planes, ch, ny, nz, scale,
    off_ref, flip_ref, feat_ref, weight_ref, bias_ref, cot_ref,
    hid_out, gin_out, gw_out,
    hid_ref, gin_ref, gw_ref, feat, weight, cot_in, send1, recv1, stag, recv2,
    zs, gz, wf, wb, shift, cot, hid, gin, gext, rs, rsr, zr, ag,
    load_sems, store_sems, send_sems, recv_sems,
):
    me, my_dp = lax.axis_index("gx"), lax.axis_index("dp")
    taps = 27
    rows = ch * planes * ny
    chunks = ny * nz // 128
    nx = n * planes
    per = rs.shape[1]

    loads = [
        pltpu.make_async_copy(source, target, load_sems.at[k])
        for k, (source, target) in enumerate(
            [(feat_ref, feat), (weight_ref, weight), (cot_ref, cot_in)]
        )
    ]
    for load in loads:
        load.start()
    stores = [
        pltpu.make_async_copy(source, target, store_sems.at[k])
        for k, (source, target) in enumerate(
            [(hid_ref, hid_out), (gin_ref, gin_out), (gw_ref, gw_out)]
        )
    ]

    barrier = pltpu.get_barrier_semaphore()

    def greet(k):
        pl.semaphore_signal(
            barrier, inc=1, device_id={"gx": wrap(me + k, n)}, device_id_type=MESH
        )

    layer, heights = 4 * dps, n // 4
    low, high = me & 3, me // 4
    mine = my_dp * 4 + low

    def layer_peer(q):
        return {"dp": q // 4, "gx": high * 4 + (q & 3)}

    def greet_layer(k):
        pl.semaphore_signal(
            barrier, inc=1, device_id=layer_peer(wrap(my_dp * 4 + 3 + k, layer)), device_id_type=MESH
        )

    each_peer(n, greet)
    each_peer(layer - 3, greet_layer)

    r_out = iota((rows, 1), 0)
    r_in = iota((1, rows), 1)
    out_c, out_y, out_x = r_out & (ch - 1), (r_out // ch) & (ny - 1), r_out // (ch * ny)
    base = (out_c * planes + out_x) * ny
    src_y = jnp.where(flip_ref[0, 1] == 1, ny - 1 - out_y, out_y) - off_ref[0, 1]
    order = one_hot(r_in == base + out_y)
    order_aug = one_hot(r_in == base + (src_y & (ny - 1)))
    zi, zo = iota((nz, 1), 0), iota((1, nz), 1)
    src_z = jnp.where(flip_ref[0, 2] == 1, nz - 1 - zo, zo) - off_ref[0, 2]
    perm_z = one_hot(zi == (src_z & (nz - 1)))
    loads[0].wait()
    local = mm(feat[...], perm_z).astype(bf16)
    local = mm(order_aug, local).astype(bf16)
    for j in range(chunks):
        y, half = j // 2, j % 2
        for x in range(planes):
            r0 = (x * ny + y) * ch
            send1[j, x] = local[r0 : r0 + ch, half * 128 : half * 128 + 128]

    pl.semaphore_wait(barrier, n - 1 + layer - 4)

    def start1(k):
        peer = wrap(me + k, n)
        pltpu.make_async_remote_copy(
            src_ref=send1.at[wrap(peer, chunks)],
            dst_ref=recv1.at[pl.ds(me * planes, planes)],
            send_sem=send_sems.at[0],
            recv_sem=recv_sems.at[0],
            device_id={"gx": peer},
            device_id_type=MESH,
        ).start()

    each_peer(n, start1)
    my_chunk = wrap(me, chunks)
    group = me // chunks * chunks
    recv1[pl.ds(me * planes, planes)] = send1[my_chunk]

    width = taps * ch
    loads[1].wait()
    tap_of = one_hot(iota((taps, 1), 0) == iota((1, width), 1) // ch)
    spread = mm(weight[...], tap_of)
    pair, lane_c = iota((ch * ch, 1), 0), iota((1, width), 1) & (ch - 1)
    by_in = jnp.where((pair & (ch - 1)) == lane_c, spread, 0.0).astype(bf16)
    by_out = jnp.where(pair // ch == lane_c, spread, 0.0).astype(bf16)
    row, across = iota((ch, 1), 0), iota((1, ch * ch), 1)
    w_fwd = mm(one_hot(row == across // ch), by_in).astype(bf16)
    w_bwd = mm(one_hot(row == (across & (ch - 1))), by_out).astype(bf16)
    bias = jnp.sum(
        jnp.where(iota((ch, 1), 0) == iota((1, ch), 1), bias_ref[...], 0.0), axis=1, keepdims=True
    )
    for k in range(9):
        wf[k] = w_fwd[:, k * 3 * ch : (k + 1) * 3 * ch]
        wb[k] = w_bwd[:, k * 3 * ch : (k + 1) * 3 * ch]
    shift[0] = one_hot(zi == ((zo - 1) & (nz - 1)))
    shift[1] = one_hot(zi == ((zo + 1) & (nz - 1)))
    loads[2].wait()
    cot[...] = mm(order, cot_in[...]).reshape(cot.shape)

    sources = []
    for p in range(chunks * planes + 2):
        target = wrap(group * planes + (p - 1), nx)
        source = jnp.where(flip_ref[0, 0] == 1, nx - 1 - target, target) - off_ref[0, 0]
        sources.append(wrap(source, nx))

    wait_bytes(recv1.at[pl.ds(0, (n - 1) * planes)], recv_sems.at[0])

    def routed(p):
        return recv1[sources[p]]

    first, last = planes + 1, planes
    for q in range(chunks):
        for x in range(planes):
            plane = routed(q * planes + x + 1)
            stag[q, x] = plane
            if x == planes - 1:
                stag[(q + 1) % chunks, first] = plane
            if x == 0:
                stag[(q - 1) % chunks, last] = plane
    stag[0, first] = routed(0)
    stag[chunks - 1, last] = routed(chunks * planes + 1)

    def start2(begin, count, k):
        q = wrap(my_chunk + k, chunks)
        pltpu.make_async_remote_copy(
            src_ref=stag.at[q, pl.ds(begin, count)],
            dst_ref=recv2.at[my_chunk, pl.ds(begin, count)],
            send_sem=send_sems.at[1 if begin == 0 else 7],
            recv_sem=recv_sems.at[1 if begin == 0 else 7],
            device_id={"gx": group + q},
            device_id_type=MESH,
        ).start()

    each_peer(chunks, functools.partial(start2, 0, planes))
    each_peer(chunks, functools.partial(start2, planes, 2))
    recv2[my_chunk] = stag[my_chunk]

    def build(target, block, slot, less):
        stacked = jnp.concatenate([block(slot, y) for y in range(ny)], axis=0)
        shifted = [
            mm(stacked, shift[less]).astype(bf16),
            stacked,
            mm(stacked, shift[1 - less]).astype(bf16),
        ]
        for y in range(ny):
            for h in range(3):
                target[slot, y, h * ch : h * ch + ch] = shifted[h][y * ch : y * ch + ch]

    def build_forward(slot, _):
        build(
            zs,
            lambda at, y: jnp.concatenate([recv2[2 * y, at], recv2[2 * y + 1, at]], axis=1),
            slot, 0,
        )
        return 0

    def build_backward(slot, _):
        build(gz, lambda at, y: gext[at, y], slot, 1)
        return 0

    def slot_of(q):
        return q % (planes + 2)

    def spread_taps(weights, source, q, sign, out):
        taps_a = [a for a in range(3) if 0 <= q + sign * (a - 1) < planes]
        stack = jnp.concatenate([weights[3 * a + e] for a in taps_a for e in range(3)], axis=0)
        for y in range(ny):
            part = mm(stack, source[slot_of(q), y])
            for k, a in enumerate(taps_a):
                for e in range(3):
                    r0 = (3 * k + e) * ch
                    key = (q + sign * (a - 1), (y + sign * (e - 1)) % ny)
                    piece = part[r0 : r0 + ch]
                    out[key] = out[key] + piece if key in out else piece

    own, halo_planes = list(range(planes)), [-1, planes]
    pre, grad_in, grads = {}, {}, {}
    wait_bytes(recv2.at[pl.ds(0, chunks - 1), pl.ds(0, planes)], recv_sems.at[1])
    for q in own:
        build_forward(q, 0)
        spread_taps(wf, zs, q, -1, pre)
    wait_bytes(recv2.at[pl.ds(0, chunks - 1), pl.ds(planes, 2)], recv_sems.at[7])
    for q in halo_planes:
        build_forward(slot_of(q), 0)
        spread_taps(wf, zs, q, -1, pre)
    grad_sum = jnp.zeros((ch, nz), f32)
    for x in range(planes):
        for y in range(ny):
            act, slope = gelu_parts(pre[x, y] + bias)
            hid[x * ny + y] = act.astype(bf16)
            grads[x, y] = (cot[x * ny + y] * slope).astype(bf16)
            gext[x, y] = grads[x, y]
            grad_sum = grad_sum + grads[x, y].astype(f32)
    sums = [jnp.zeros((3 * ch, 3 * ch), f32) for _ in range(3)]
    for q in own + halo_planes:
        taps_a = [a for a in range(3) if 0 <= q - a + 1 < planes]
        for y in range(ny):
            stack = jnp.concatenate(
                [gext[q - a + 1, (y - e + 1) % ny] for a in taps_a for e in range(3)], axis=0
            )
            part = mm_t(stack, zs[slot_of(q), y])
            for k, a in enumerate(taps_a):
                sums[a] = sums[a] + part[k * 3 * ch : (k + 1) * 3 * ch]

    right, left = lax.rem(me + 1, n), lax.rem(me + n - 1, n)
    halos = [
        pltpu.make_async_remote_copy(
            src_ref=gext.at[here],
            dst_ref=gext.at[there],
            send_sem=send_sems.at[2 + side],
            recv_sem=recv_sems.at[2 + side],
            device_id={"gx": peer},
            device_id_type=MESH,
        )
        for side, (here, there, peer) in enumerate(
            [(planes - 1, planes + 1, right), (0, planes, left)]
        )
    ]
    gw = jnp.concatenate(
        [sums[a][e * ch : e * ch + ch] for a in range(3) for e in range(3)]
        + [jnp.sum(grad_sum, axis=1, keepdims=True), jnp.zeros((ch, 511 - width), f32)],
        axis=1,
    )
    groups = ch // per
    for k in range(layer):
        g, q = k % groups, k // groups
        rs[k] = gw[g * per : g * per + per, q * 128 : q * 128 + 128]

    def start_rs(k):
        peer = wrap(mine + k, layer)
        pltpu.make_async_remote_copy(
            src_ref=rs.at[peer],
            dst_ref=rsr.at[mine],
            send_sem=send_sems.at[4],
            recv_sem=recv_sems.at[4],
            device_id=layer_peer(peer),
            device_id_type=MESH,
        ).start()

    each_peer(layer, start_rs)
    rsr[mine] = rs[mine]
    for halo in halos:
        halo.start()

    b_out, b_in = iota((rows, 1), 0), iota((1, rows), 1)
    b_base = ((b_in & (ch - 1)) * planes + b_in // (ch * ny)) * ny
    back = one_hot(b_out == b_base + ((b_in // ch) & (ny - 1)))
    hid_ref[...] = mm(back, hid[...].reshape(rows, nz)).astype(bf16)
    stores[0].start()

    for q in own:
        build_backward(q, 0)
        spread_taps(wb, gz, q, 1, grad_in)

    wait_bytes(rsr.at[pl.ds(0, layer - 1)], recv_sems.at[4])
    total = rsr[0]
    for k in range(1, layer):
        total = total + rsr[k]
    zr[high] = total

    def start_z(k):
        pltpu.make_async_remote_copy(
            src_ref=zr.at[high],
            dst_ref=zr.at[high],
            send_sem=send_sems.at[5],
            recv_sem=recv_sems.at[5],
            device_id={"gx": wrap(high + k, heights) * 4 + low},
            device_id_type=MESH,
        ).start()

    each_peer(heights, start_z)

    for halo in halos:
        halo.wait()
    for q in halo_planes:
        build_backward(slot_of(q), 0)

    wait_bytes(zr.at[pl.ds(0, heights - 1)], recv_sems.at[5])
    total = zr[0]
    for k in range(1, heights):
        total = total + zr[k]
    ag[mine] = total * scale

    def start_ag(k):
        pltpu.make_async_remote_copy(
            src_ref=ag.at[mine],
            dst_ref=ag.at[mine],
            send_sem=send_sems.at[6],
            recv_sem=recv_sems.at[6],
            device_id=layer_peer(wrap(mine + k, layer)),
            device_id_type=MESH,
        ).start()

    each_peer(layer, start_ag)

    for q in halo_planes:
        spread_taps(wb, gz, q, 1, grad_in)
    for x in range(planes):
        for y in range(ny):
            gin[x * ny + y] = grad_in[x, y].astype(bf16)
    gin_ref[...] = mm(back, gin[...].reshape(rows, nz)).astype(bf16)

    stores[1].start()
    wait_bytes(ag.at[pl.ds(0, layer - 1)], recv_sems.at[6])
    for k in range(layer):
        g, q = k % groups, k // groups
        gw_ref[g * per : g * per + per, q * 128 : q * 128 + 128] = ag[k]

    stores[2].start()
    wait_bytes(recv1.at[pl.ds(0, (n - 1) * planes)], send_sems.at[0])
    wait_bytes(recv2.at[pl.ds(0, chunks - 1), pl.ds(0, planes)], send_sems.at[1])
    wait_bytes(recv2.at[pl.ds(0, chunks - 1), pl.ds(planes, 2)], send_sems.at[7])
    wait_bytes(rsr.at[pl.ds(0, layer - 1)], send_sems.at[4])
    wait_bytes(zr.at[pl.ds(0, heights - 1)], send_sems.at[5])
    wait_bytes(ag.at[pl.ds(0, layer - 1)], send_sems.at[6])
    for store in stores:
        store.wait()


def finish(
    ch, taps, hid_in, gin_in, gw_in, hid_out, gin_out, gw_out, gb_out,
    gw_ref, hid, gin, gw, gb, load_sems, sems,
):
    width = taps * ch
    loads = [
        pltpu.make_async_copy(source, target, load_sems.at[k])
        for k, (source, target) in enumerate([(hid_in, hid), (gin_in, gin), (gw_in, gw_ref)])
    ]
    for k in (2, 0, 1):
        loads[k].start()
    stores = [
        pltpu.make_async_copy(source, target, sems.at[k])
        for k, (source, target) in enumerate(
            [(hid, hid_out), (gin, gin_out), (gw, gw_out), (gb, gb_out)]
        )
    ]
    kept = iota((ch, 1), 0) == (iota((1, width), 1) & (ch - 1))
    tap_of = one_hot(iota((width, 1), 0) // ch == iota((1, taps), 1))
    for k in (2, 0, 1):
        loads[k].wait()
    stores[0].start()
    stores[1].start()
    pairs = jnp.concatenate(
        [jnp.where(kept, gw_ref[o : o + 1, 0:width], 0.0) for o in range(ch)], axis=0
    )
    high = pairs.astype(bf16)
    rest = pairs - high.astype(f32)
    mid = rest.astype(bf16)
    low = (rest - mid.astype(f32)).astype(bf16)
    gw[...] = mm(high, tap_of) + (mm(mid, tap_of) + mm(low, tap_of))
    stores[2].start()
    gb[...] = jnp.sum(
        jnp.where(iota((ch, 1), 0) == iota((1, ch), 1), gw_ref[:, width : width + 1], 0.0),
        axis=0, keepdims=True,
    )
    stores[3].start()
    for store in stores:
        store.wait()


def on_device(features, offsets, flip_bits, weight, conv_bias, cotangent):
    _, ch, planes, ny, nz = features.shape
    n, dps = lax.axis_size("gx"), lax.axis_size("dp")
    taps = weight.shape[0]
    rows, cells, chunks = ch * planes * ny, planes * ny * nz, ny * nz // 128
    width = taps * ch
    layer = 4 * dps
    per = ch * 512 // (128 * layer)
    scale = 1.0 / math.sqrt(dps * n * cells)
    vmem = pl.BlockSpec(memory_space=pltpu.VMEM)
    smem = pl.BlockSpec(memory_space=pltpu.SMEM)
    hbm = pl.BlockSpec(memory_space=pltpu.HBM)
    hidden, grad_in, grad_w = pl.pallas_call(
        functools.partial(kernel, n, dps, planes, ch, ny, nz, scale),
        out_shape=(
            jax.ShapeDtypeStruct((rows, nz), bf16),
            jax.ShapeDtypeStruct((rows, nz), bf16),
            jax.ShapeDtypeStruct((ch, 512), f32),
        ),
        in_specs=[smem, smem, hbm, hbm, vmem, hbm],
        out_specs=(hbm, hbm, hbm),
        scratch_shapes=[
            pltpu.VMEM((rows, nz), bf16),
            pltpu.VMEM((rows, nz), bf16),
            pltpu.VMEM((ch, 512), f32),
            pltpu.VMEM((rows, nz), bf16),
            pltpu.VMEM((ch * ch, taps), bf16),
            pltpu.VMEM((rows, nz), bf16),
            pltpu.VMEM((chunks, planes, ch, 128), bf16),
            pltpu.VMEM((n * planes, ch, 128), bf16),
            pltpu.VMEM((chunks, planes + 2, ch, 128), bf16),
            pltpu.VMEM((chunks, planes + 2, ch, 128), bf16),
            pltpu.VMEM((planes + 2, ny, 3 * ch, nz), bf16),
            pltpu.VMEM((planes + 2, ny, 3 * ch, nz), bf16),
            pltpu.VMEM((9, ch, 3 * ch), bf16),
            pltpu.VMEM((9, ch, 3 * ch), bf16),
            pltpu.VMEM((2, nz, nz), bf16),
            pltpu.VMEM((planes * ny, ch, nz), f32),
            pltpu.VMEM((planes * ny, ch, nz), bf16),
            pltpu.VMEM((planes * ny, ch, nz), bf16),
            pltpu.VMEM((planes + 2, ny, ch, nz), bf16),
            pltpu.VMEM((layer, per, 128), f32),
            pltpu.VMEM((layer, per, 128), f32),
            pltpu.VMEM((n // 4, per, 128), f32),
            pltpu.VMEM((layer, per, 128), f32),
            pltpu.SemaphoreType.DMA((3,)),
            pltpu.SemaphoreType.DMA((3,)),
            pltpu.SemaphoreType.DMA((8,)),
            pltpu.SemaphoreType.DMA((8,)),
        ],
        compiler_params=pltpu.CompilerParams(
            collective_id=0, has_side_effects=True, vmem_limit_bytes=63 * 2**20
        ),
        cost_estimate=pl.CostEstimate(
            flops=6 * ch * width * cells, bytes_accessed=8 * rows * nz, transcendentals=2 * ch * cells
        ),
    )(
        offsets,
        flip_bits,
        features.reshape(rows, nz),
        weight.transpose(1, 2, 0).reshape(ch * ch, taps),
        conv_bias.reshape(1, ch),
        cotangent.reshape(rows, nz),
    )
    hidden, grad_in, grad_w, grad_b = pl.pallas_call(
        functools.partial(finish, ch, taps),
        out_shape=(
            jax.ShapeDtypeStruct((rows, nz), bf16),
            jax.ShapeDtypeStruct((rows, nz), bf16),
            jax.ShapeDtypeStruct((ch * ch, taps), f32),
            jax.ShapeDtypeStruct((1, ch), f32),
        ),
        in_specs=[hbm, hbm, hbm],
        out_specs=(hbm, hbm, hbm, hbm),
        scratch_shapes=[
            pltpu.VMEM((ch, 512), f32),
            pltpu.VMEM((rows, nz), bf16),
            pltpu.VMEM((rows, nz), bf16),
            pltpu.VMEM((ch * ch, taps), f32),
            pltpu.VMEM((1, ch), f32),
            pltpu.SemaphoreType.DMA((3,)),
            pltpu.SemaphoreType.DMA((4,)),
        ],
        compiler_params=pltpu.CompilerParams(vmem_limit_bytes=63 * 2**20),
    )(hidden, grad_in, grad_w)
    return (
        hidden.reshape(features.shape),
        grad_in.reshape(features.shape),
        grad_w.reshape(ch, ch, taps).transpose(2, 0, 1),
        grad_b.reshape(ch),
    )


def solution(mesh):
    in_specs = (
        P("dp", None, "gx", None, None),
        P("dp", None),
        P("dp", None),
        P(),
        P(),
        P("dp", None, "gx", None, None),
    )
    out_specs = (P("dp", None, "gx", None, None), P("dp", None, "gx", None, None), P(), P())
    return jax.shard_map(
        on_device, mesh=mesh, in_specs=in_specs, out_specs=out_specs, check_vma=False
    )
```

```python
import functools
import math

import jax
import jax.numpy as jnp
from jax import lax
from jax.experimental import pallas as pl
from jax.experimental.pallas import tpu as pltpu
from jax.sharding import PartitionSpec as P

MESH = pl.DeviceIdType.MESH
bf16, f32 = jnp.bfloat16, jnp.float32


def iota(shape, dim):
    return lax.broadcasted_iota(jnp.int32, shape, dim)


def one_hot(mask):
    return jnp.where(mask, 1.0, 0.0).astype(bf16)


def mm(a, b):
    return jnp.dot(a, b, preferred_element_type=f32)


def mm_t(a, b):
    return lax.dot_general(a, b, (((1,), (1,)), ((), ())), preferred_element_type=f32)


def gelu_parts(pre_act):
    normal_cdf = 0.5 * (1.0 + lax.erf(pre_act * 0.7071067811865476))
    density = jnp.exp(-0.5 * pre_act * pre_act) * 0.3989422804014327
    return (pre_act * normal_cdf, normal_cdf + pre_act * density)


def wrap(index, count):
    if count & (count - 1) == 0:
        return index & (count - 1)
    return lax.rem(index + count, count)


def each_peer(count, body):
    lax.fori_loop(1, count, lambda k, _: body(k) or 0, 0, unroll=count <= 16)


def wait_bytes(ref, sem):
    pltpu.make_async_copy(ref, ref, sem).wait()


def kernel(
    n, dps, planes, ch, ny, nz, scale,
    off_ref, flip_ref, feat_ref, weight_ref, bias_ref, cot_ref,
    hid_out, gin_out, gw_out,
    hid_ref, gin_ref, gw_ref, feat, weight, cot_in, send1, recv1, stag, recv2,
    zs, gz, wf, wb, shift, cot, hid, gin, gext, rs, rsr, zr, ag,
    load_sems, store_sems, send_sems, recv_sems,
):
    me, my_dp = lax.axis_index("gx"), lax.axis_index("dp")
    taps = 27
    rows = ch * planes * ny
    chunks = ny * nz // 128
    nx = n * planes
    per = rs.shape[1]

    loads = [
        pltpu.make_async_copy(source, target, load_sems.at[k])
        for k, (source, target) in enumerate(
            [(feat_ref, feat), (weight_ref, weight), (cot_ref, cot_in)]
        )
    ]
    for load in loads:
        load.start()
    stores = [
        pltpu.make_async_copy(source, target, store_sems.at[k])
        for k, (source, target) in enumerate(
            [(hid_ref, hid_out), (gin_ref, gin_out), (gw_ref, gw_out)]
        )
    ]

    barrier = pltpu.get_barrier_semaphore()

    def greet(k):
        pl.semaphore_signal(
            barrier, inc=1, device_id={"gx": wrap(me + k, n)}, device_id_type=MESH
        )

    layer, heights = 4 * dps, n // 4
    low, high = me & 3, me // 4
    mine = my_dp * 4 + low

    def layer_peer(q):
        return {"dp": q // 4, "gx": high * 4 + (q & 3)}

    def greet_layer(k):
        pl.semaphore_signal(
            barrier, inc=1, device_id=layer_peer(wrap(my_dp * 4 + 3 + k, layer)), device_id_type=MESH
        )

    each_peer(n, greet)
    each_peer(layer - 3, greet_layer)

    r_out = iota((rows, 1), 0)
    r_in = iota((1, rows), 1)
    out_c, out_y, out_x = r_out & (ch - 1), (r_out // ch) & (ny - 1), r_out // (ch * ny)
    base = (out_c * planes + out_x) * ny
    src_y = jnp.where(flip_ref[0, 1] == 1, ny - 1 - out_y, out_y) - off_ref[0, 1]
    order = one_hot(r_in == base + out_y)
    order_aug = one_hot(r_in == base + (src_y & (ny - 1)))
    zi, zo = iota((nz, 1), 0), iota((1, nz), 1)
    src_z = jnp.where(flip_ref[0, 2] == 1, nz - 1 - zo, zo) - off_ref[0, 2]
    perm_z = one_hot(zi == (src_z & (nz - 1)))
    loads[0].wait()
    local = mm(feat[...], perm_z).astype(bf16)
    local = mm(order_aug, local).astype(bf16)
    for j in range(chunks):
        y, half = j // 2, j % 2
        for x in range(planes):
            r0 = (x * ny + y) * ch
            send1[j, x] = local[r0 : r0 + ch, half * 128 : half * 128 + 128]

    pl.semaphore_wait(barrier, n - 1 + layer - 4)

    def start1(k):
        peer = wrap(me + k, n)
        pltpu.make_async_remote_copy(
            src_ref=send1.at[wrap(peer, chunks)],
            dst_ref=recv1.at[pl.ds(me * planes, planes)],
            send_sem=send_sems.at[0],
            recv_sem=recv_sems.at[0],
            device_id={"gx": peer},
            device_id_type=MESH,
        ).start()

    each_peer(n, start1)
    my_chunk = wrap(me, chunks)
    group = me // chunks * chunks
    recv1[pl.ds(me * planes, planes)] = send1[my_chunk]

    width = taps * ch
    loads[1].wait()
    tap_of = one_hot(iota((taps, 1), 0) == iota((1, width), 1) // ch)
    spread = mm(weight[...], tap_of)
    pair, lane_c = iota((ch * ch, 1), 0), iota((1, width), 1) & (ch - 1)
    by_in = jnp.where((pair & (ch - 1)) == lane_c, spread, 0.0).astype(bf16)
    by_out = jnp.where(pair // ch == lane_c, spread, 0.0).astype(bf16)
    row, across = iota((ch, 1), 0), iota((1, ch * ch), 1)
    w_fwd = mm(one_hot(row == across // ch), by_in).astype(bf16)
    w_bwd = mm(one_hot(row == (across & (ch - 1))), by_out).astype(bf16)
    bias = jnp.sum(
        jnp.where(iota((ch, 1), 0) == iota((1, ch), 1), bias_ref[...], 0.0), axis=1, keepdims=True
    )
    for k in range(9):
        wf[k] = w_fwd[:, k * 3 * ch : (k + 1) * 3 * ch]
        wb[k] = w_bwd[:, k * 3 * ch : (k + 1) * 3 * ch]
    shift[0] = one_hot(zi == ((zo - 1) & (nz - 1)))
    shift[1] = one_hot(zi == ((zo + 1) & (nz - 1)))
    loads[2].wait()
    cot[...] = mm(order, cot_in[...]).reshape(cot.shape)

    sources = []
    for p in range(chunks * planes + 2):
        target = wrap(group * planes + (p - 1), nx)
        source = jnp.where(flip_ref[0, 0] == 1, nx - 1 - target, target) - off_ref[0, 0]
        sources.append(wrap(source, nx))

    wait_bytes(recv1.at[pl.ds(0, (n - 1) * planes)], recv_sems.at[0])

    def routed(p):
        return recv1[sources[p]]

    first, last = planes + 1, planes
    for q in range(chunks):
        for x in range(planes):
            plane = routed(q * planes + x + 1)
            stag[q, x] = plane
            if x == planes - 1:
                stag[(q + 1) % chunks, first] = plane
            if x == 0:
                stag[(q - 1) % chunks, last] = plane
    stag[0, first] = routed(0)
    stag[chunks - 1, last] = routed(chunks * planes + 1)

    def start2(begin, count, k):
        q = wrap(my_chunk + k, chunks)
        pltpu.make_async_remote_copy(
            src_ref=stag.at[q, pl.ds(begin, count)],
            dst_ref=recv2.at[my_chunk, pl.ds(begin, count)],
            send_sem=send_sems.at[1 if begin == 0 else 7],
            recv_sem=recv_sems.at[1 if begin == 0 else 7],
            device_id={"gx": group + q},
            device_id_type=MESH,
        ).start()

    each_peer(chunks, functools.partial(start2, 0, planes))
    each_peer(chunks, functools.partial(start2, planes, 2))
    recv2[my_chunk] = stag[my_chunk]

    def build(target, block, slot, less):
        stacked = jnp.concatenate([block(slot, y) for y in range(ny)], axis=0)
        shifted = [
            mm(stacked, shift[less]).astype(bf16),
            stacked,
            mm(stacked, shift[1 - less]).astype(bf16),
        ]
        for y in range(ny):
            for h in range(3):
                target[slot, y, h * ch : h * ch + ch] = shifted[h][y * ch : y * ch + ch]

    def build_forward(slot, _):
        build(
            zs,
            lambda at, y: jnp.concatenate([recv2[2 * y, at], recv2[2 * y + 1, at]], axis=1),
            slot, 0,
        )
        return 0

    def build_backward(slot, _):
        build(gz, lambda at, y: gext[at, y], slot, 1)
        return 0

    def slot_of(q):
        return q % (planes + 2)

    def spread_taps(weights, source, q, sign, out):
        taps_a = [a for a in range(3) if 0 <= q + sign * (a - 1) < planes]
        stack = jnp.concatenate([weights[3 * a + e] for a in taps_a for e in range(3)], axis=0)
        for y in range(ny):
            part = mm(stack, source[slot_of(q), y])
            for k, a in enumerate(taps_a):
                for e in range(3):
                    r0 = (3 * k + e) * ch
                    key = (q + sign * (a - 1), (y + sign * (e - 1)) % ny)
                    piece = part[r0 : r0 + ch]
                    out[key] = out[key] + piece if key in out else piece

    own, halo_planes = list(range(planes)), [-1, planes]
    pre, grad_in, grads = {}, {}, {}
    wait_bytes(recv2.at[pl.ds(0, chunks - 1), pl.ds(0, planes)], recv_sems.at[1])
    for q in own:
        build_forward(q, 0)
        spread_taps(wf, zs, q, -1, pre)
    wait_bytes(recv2.at[pl.ds(0, chunks - 1), pl.ds(planes, 2)], recv_sems.at[7])
    for q in halo_planes:
        build_forward(slot_of(q), 0)
        spread_taps(wf, zs, q, -1, pre)
    grad_sum = jnp.zeros((ch, nz), f32)
    for x in range(planes):
        for y in range(ny):
            act, slope = gelu_parts(pre[x, y] + bias)
            hid[x * ny + y] = act.astype(bf16)
            grads[x, y] = (cot[x * ny + y] * slope).astype(bf16)
            gext[x, y] = grads[x, y]
            grad_sum = grad_sum + grads[x, y].astype(f32)
    right, left = lax.rem(me + 1, n), lax.rem(me + n - 1, n)
    halos = [
        pltpu.make_async_remote_copy(
            src_ref=gext.at[here],
            dst_ref=gext.at[there],
            send_sem=send_sems.at[2 + side],
            recv_sem=recv_sems.at[2 + side],
            device_id={"gx": peer},
            device_id_type=MESH,
        )
        for side, (here, there, peer) in enumerate(
            [(planes - 1, planes + 1, right), (0, planes, left)]
        )
    ]
    for halo in halos:
        halo.start()

    sums = [jnp.zeros((3 * ch, 3 * ch), f32) for _ in range(3)]
    for q in own + halo_planes:
        taps_a = [a for a in range(3) if 0 <= q - a + 1 < planes]
        for y in range(ny):
            stack = jnp.concatenate(
                [gext[q - a + 1, (y - e + 1) % ny] for a in taps_a for e in range(3)], axis=0
            )
            part = mm_t(stack, zs[slot_of(q), y])
            for k, a in enumerate(taps_a):
                sums[a] = sums[a] + part[k * 3 * ch : (k + 1) * 3 * ch]
    gw = jnp.concatenate(
        [sums[a][e * ch : e * ch + ch] for a in range(3) for e in range(3)]
        + [jnp.sum(grad_sum, axis=1, keepdims=True), jnp.zeros((ch, 511 - width), f32)],
        axis=1,
    )
    groups = ch // per
    for k in range(layer):
        g, q = k % groups, k // groups
        rs[k] = gw[g * per : g * per + per, q * 128 : q * 128 + 128]

    def start_rs(k):
        peer = wrap(mine + k, layer)
        pltpu.make_async_remote_copy(
            src_ref=rs.at[peer],
            dst_ref=rsr.at[mine],
            send_sem=send_sems.at[4],
            recv_sem=recv_sems.at[4],
            device_id=layer_peer(peer),
            device_id_type=MESH,
        ).start()

    each_peer(layer, start_rs)
    rsr[mine] = rs[mine]

    b_out, b_in = iota((rows, 1), 0), iota((1, rows), 1)
    b_base = ((b_in & (ch - 1)) * planes + b_in // (ch * ny)) * ny
    back = one_hot(b_out == b_base + ((b_in // ch) & (ny - 1)))
    hid_ref[...] = mm(back, hid[...].reshape(rows, nz)).astype(bf16)
    stores[0].start()

    for q in own:
        build_backward(q, 0)
        spread_taps(wb, gz, q, 1, grad_in)

    wait_bytes(rsr.at[pl.ds(0, layer - 1)], recv_sems.at[4])
    total = rsr[0]
    for k in range(1, layer):
        total = total + rsr[k]
    zr[high] = total

    def start_z(k):
        pltpu.make_async_remote_copy(
            src_ref=zr.at[high],
            dst_ref=zr.at[high],
            send_sem=send_sems.at[5],
            recv_sem=recv_sems.at[5],
            device_id={"gx": wrap(high + k, heights) * 4 + low},
            device_id_type=MESH,
        ).start()

    each_peer(heights, start_z)

    for halo in halos:
        halo.wait()
    for q in halo_planes:
        build_backward(slot_of(q), 0)

    wait_bytes(zr.at[pl.ds(0, heights - 1)], recv_sems.at[5])
    total = zr[0]
    for k in range(1, heights):
        total = total + zr[k]
    ag[mine] = total * scale

    def start_ag(k):
        pltpu.make_async_remote_copy(
            src_ref=ag.at[mine],
            dst_ref=ag.at[mine],
            send_sem=send_sems.at[6],
            recv_sem=recv_sems.at[6],
            device_id=layer_peer(wrap(mine + k, layer)),
            device_id_type=MESH,
        ).start()

    each_peer(layer, start_ag)

    for q in halo_planes:
        spread_taps(wb, gz, q, 1, grad_in)
    for x in range(planes):
        for y in range(ny):
            gin[x * ny + y] = grad_in[x, y].astype(bf16)
    gin_ref[...] = mm(back, gin[...].reshape(rows, nz)).astype(bf16)

    stores[1].start()
    wait_bytes(ag.at[pl.ds(0, layer - 1)], recv_sems.at[6])
    for k in range(layer):
        g, q = k % groups, k // groups
        gw_ref[g * per : g * per + per, q * 128 : q * 128 + 128] = ag[k]

    stores[2].start()
    wait_bytes(recv1.at[pl.ds(0, (n - 1) * planes)], send_sems.at[0])
    wait_bytes(recv2.at[pl.ds(0, chunks - 1), pl.ds(0, planes)], send_sems.at[1])
    wait_bytes(recv2.at[pl.ds(0, chunks - 1), pl.ds(planes, 2)], send_sems.at[7])
    wait_bytes(rsr.at[pl.ds(0, layer - 1)], send_sems.at[4])
    wait_bytes(zr.at[pl.ds(0, heights - 1)], send_sems.at[5])
    wait_bytes(ag.at[pl.ds(0, layer - 1)], send_sems.at[6])
    for store in stores:
        store.wait()


def finish(
    ch, taps, hid_in, gin_in, gw_in, hid_out, gin_out, gw_out, gb_out,
    gw_ref, hid, gin, gw, gb, load_sems, sems,
):
    width = taps * ch
    loads = [
        pltpu.make_async_copy(source, target, load_sems.at[k])
        for k, (source, target) in enumerate([(hid_in, hid), (gin_in, gin), (gw_in, gw_ref)])
    ]
    for k in (2, 0, 1):
        loads[k].start()
    stores = [
        pltpu.make_async_copy(source, target, sems.at[k])
        for k, (source, target) in enumerate(
            [(hid, hid_out), (gin, gin_out), (gw, gw_out), (gb, gb_out)]
        )
    ]
    kept = iota((ch, 1), 0) == (iota((1, width), 1) & (ch - 1))
    tap_of = one_hot(iota((width, 1), 0) // ch == iota((1, taps), 1))
    for k in (2, 0, 1):
        loads[k].wait()
    stores[0].start()
    stores[1].start()
    pairs = jnp.concatenate(
        [jnp.where(kept, gw_ref[o : o + 1, 0:width], 0.0) for o in range(ch)], axis=0
    )
    high = pairs.astype(bf16)
    rest = pairs - high.astype(f32)
    mid = rest.astype(bf16)
    low = (rest - mid.astype(f32)).astype(bf16)
    gw[...] = mm(high, tap_of) + (mm(mid, tap_of) + mm(low, tap_of))
    stores[2].start()
    gb[...] = jnp.sum(
        jnp.where(iota((ch, 1), 0) == iota((1, ch), 1), gw_ref[:, width : width + 1], 0.0),
        axis=0, keepdims=True,
    )
    stores[3].start()
    for store in stores:
        store.wait()


def on_device(features, offsets, flip_bits, weight, conv_bias, cotangent):
    _, ch, planes, ny, nz = features.shape
    n, dps = lax.axis_size("gx"), lax.axis_size("dp")
    taps = weight.shape[0]
    rows, cells, chunks = ch * planes * ny, planes * ny * nz, ny * nz // 128
    width = taps * ch
    layer = 4 * dps
    per = ch * 512 // (128 * layer)
    scale = 1.0 / math.sqrt(dps * n * cells)
    vmem = pl.BlockSpec(memory_space=pltpu.VMEM)
    smem = pl.BlockSpec(memory_space=pltpu.SMEM)
    hbm = pl.BlockSpec(memory_space=pltpu.HBM)
    hidden, grad_in, grad_w = pl.pallas_call(
        functools.partial(kernel, n, dps, planes, ch, ny, nz, scale),
        out_shape=(
            jax.ShapeDtypeStruct((rows, nz), bf16),
            jax.ShapeDtypeStruct((rows, nz), bf16),
            jax.ShapeDtypeStruct((ch, 512), f32),
        ),
        in_specs=[smem, smem, hbm, hbm, vmem, hbm],
        out_specs=(hbm, hbm, hbm),
        scratch_shapes=[
            pltpu.VMEM((rows, nz), bf16),
            pltpu.VMEM((rows, nz), bf16),
            pltpu.VMEM((ch, 512), f32),
            pltpu.VMEM((rows, nz), bf16),
            pltpu.VMEM((ch * ch, taps), bf16),
            pltpu.VMEM((rows, nz), bf16),
            pltpu.VMEM((chunks, planes, ch, 128), bf16),
            pltpu.VMEM((n * planes, ch, 128), bf16),
            pltpu.VMEM((chunks, planes + 2, ch, 128), bf16),
            pltpu.VMEM((chunks, planes + 2, ch, 128), bf16),
            pltpu.VMEM((planes + 2, ny, 3 * ch, nz), bf16),
            pltpu.VMEM((planes + 2, ny, 3 * ch, nz), bf16),
            pltpu.VMEM((9, ch, 3 * ch), bf16),
            pltpu.VMEM((9, ch, 3 * ch), bf16),
            pltpu.VMEM((2, nz, nz), bf16),
            pltpu.VMEM((planes * ny, ch, nz), f32),
            pltpu.VMEM((planes * ny, ch, nz), bf16),
            pltpu.VMEM((planes * ny, ch, nz), bf16),
            pltpu.VMEM((planes + 2, ny, ch, nz), bf16),
            pltpu.VMEM((layer, per, 128), f32),
            pltpu.VMEM((layer, per, 128), f32),
            pltpu.VMEM((n // 4, per, 128), f32),
            pltpu.VMEM((layer, per, 128), f32),
            pltpu.SemaphoreType.DMA((3,)),
            pltpu.SemaphoreType.DMA((3,)),
            pltpu.SemaphoreType.DMA((8,)),
            pltpu.SemaphoreType.DMA((8,)),
        ],
        compiler_params=pltpu.CompilerParams(
            collective_id=0, has_side_effects=True, vmem_limit_bytes=63 * 2**20
        ),
        cost_estimate=pl.CostEstimate(
            flops=6 * ch * width * cells, bytes_accessed=8 * rows * nz, transcendentals=2 * ch * cells
        ),
    )(
        offsets,
        flip_bits,
        features.reshape(rows, nz),
        weight.transpose(1, 2, 0).reshape(ch * ch, taps),
        conv_bias.reshape(1, ch),
        cotangent.reshape(rows, nz),
    )
    hidden, grad_in, grad_w, grad_b = pl.pallas_call(
        functools.partial(finish, ch, taps),
        out_shape=(
            jax.ShapeDtypeStruct((rows, nz), bf16),
            jax.ShapeDtypeStruct((rows, nz), bf16),
            jax.ShapeDtypeStruct((ch * ch, taps), f32),
            jax.ShapeDtypeStruct((1, ch), f32),
        ),
        in_specs=[hbm, hbm, hbm],
        out_specs=(hbm, hbm, hbm, hbm),
        scratch_shapes=[
            pltpu.VMEM((ch, 512), f32),
            pltpu.VMEM((rows, nz), bf16),
            pltpu.VMEM((rows, nz), bf16),
            pltpu.VMEM((ch * ch, taps), f32),
            pltpu.VMEM((1, ch), f32),
            pltpu.SemaphoreType.DMA((3,)),
            pltpu.SemaphoreType.DMA((4,)),
        ],
        compiler_params=pltpu.CompilerParams(vmem_limit_bytes=63 * 2**20),
    )(hidden, grad_in, grad_w)
    return (
        hidden.reshape(features.shape),
        grad_in.reshape(features.shape),
        grad_w.reshape(ch, ch, taps).transpose(2, 0, 1),
        grad_b.reshape(ch),
    )


def solution(mesh):
    in_specs = (
        P("dp", None, "gx", None, None),
        P("dp", None),
        P("dp", None),
        P(),
        P(),
        P("dp", None, "gx", None, None),
    )
    out_specs = (P("dp", None, "gx", None, None), P("dp", None, "gx", None, None), P(), P())
    return jax.shard_map(
        on_device, mesh=mesh, in_specs=in_specs, out_specs=out_specs, check_vma=False
    )
```
